128 devices in a mesh: row: 16 (over z_lo, x, core), col: 8 (over y, z_hi).
Axes of the slice: x: 4, y: 4, z: 4 (z_hi: 2, z_lo: 2; z = z_hi * 2 + z_lo), core: 2. Of those that a mesh axis runs over, the one named last changes fastest.
Arguments:
- image: bfloat16 [128, 512, 256], P('row', 'col'), may hold values from -6 to 6
- gain_fine: float32 [256], replicated, may hold values from 0.1 to 1.9
- qkv_fine: bfloat16 [256, 768], replicated, as said below
- out_fine: bfloat16 [256, 256], replicated, may hold values from -0.375 to 0.375
- merge_fine: bfloat16 [1024, 512], replicated, may hold values from -0.1875 to 0.1875
- gain_mid: float32 [512], replicated, may hold values from 0.1 to 1.9
- qkv_mid: bfloat16 [512, 1536], replicated, as said below
- out_mid: bfloat16 [512, 512], replicated, may hold values from -0.25 to 0.25
- merge_mid: bfloat16 [2048, 1024], replicated, may hold values from -0.125 to 0.125
- gain_coarse: float32 [1024], replicated, may hold values from 0.1 to 1.9
- qkv_coarse: bfloat16 [1024, 3072], replicated, as said below
- out_coarse: bfloat16 [1024, 1024], replicated, may hold values from -0.1875 to 0.1875
Outputs:
- skip_fine: bfloat16 [128, 512, 256], P('row', 'col')
- skip_mid: bfloat16 [64, 256, 512], P('row', 'col')
- coarse_out: bfloat16 [32, 128, 1024], P('row', 'col')
The draws below stay inside these ranges and needn't reach their ends.
Inputs may be any that keep to these rules, and one draw needn't show every extreme that they name: `qkv_fine`: query, key and value projections side by side. `qkv_mid`: query, key and value projections side by side. `qkv_coarse`: query, key and value projections side by side.
All inputs are finite; a program needn't handle non-finite values.
Results may differ from the reference program's by a relative error of at most 0.025.
Values may be sent and summed in bfloat16 or wider, within the bound.
A program may use at most 192 MiB of HBM per device.

```python
import math
import jax
import jax.numpy as jnp
from jax import lax

W1 = 256
W2 = 512
W3 = 1024
HEAD = 64
ROWS = 128
COLS = 512


def projection_draw(key, channels):
    keys = jax.random.split(key, 4)
    query_part = jax.random.normal(keys[1], (channels, channels), jnp.float32)
    key_part = jax.random.normal(keys[2], (channels, channels), jnp.float32)
    value_part = jax.random.normal(keys[3], (channels, channels), jnp.float32)
    joined = jnp.concatenate([query_part, key_part, value_part], axis=1)
    return (joined * channels ** (-0.5)).astype(jnp.bfloat16)


def draw_qkv_fine(key, part):
    key = jax.random.fold_in(key, 11)
    return projection_draw(key, W1)


def draw_qkv_mid(key, part):
    key = jax.random.fold_in(key, 12)
    return projection_draw(key, W2)


def draw_qkv_coarse(key, part):
    key = jax.random.fold_in(key, 13)
    return projection_draw(key, W3)


def level_of(rng, shape, cuts, low, top_value):
    def one(dim, parts):
        draws = jax.random.uniform(jax.random.fold_in(jax.random.fold_in(rng, 6), dim), (parts,), jnp.float32, low / len(cuts), top_value / len(cuts))
        return jnp.repeat(jnp.exp(draws), shape[dim] // parts).reshape((-1,) + (1,) * (len(shape) - dim - 1))

    factor_of = one(*cuts[0])
    for cut in cuts[1:]:
        factor_of = factor_of * one(*cut)
    return factor_of


def scatter_about(key, shape, spread, bound, cuts=(), kind=jnp.bfloat16):
    array = jax.random.normal(key, shape, jnp.float32) * spread
    if len(cuts) > 0:
        array = level_of(key, shape, cuts, -0.22, 0.18) * array
    return jnp.clip(array, min=-bound, max=bound).astype(kind)


def setup_inputs(seed: int = 0) -> dict:
    seeds = jax.random.split(jax.random.key(seed), 13)
    return {
        "image": scatter_about(seeds[0], (ROWS, COLS, W1), 1.0, 6.0, ((0, 16), (1, 8))),
        "gain_fine": jnp.clip(1.0 + 0.18 * jax.random.normal(seeds[1], (W1,), jnp.float32), 0.1, 1.9),
        "qkv_fine": draw_qkv_fine(jax.random.fold_in(seeds[12], 71), 0),
        "out_fine": scatter_about(seeds[3], (W1, W1), W1 ** -0.5, 0.375),
        "merge_fine": scatter_about(seeds[4], (4 * W1, W2), (4 * W1) ** -0.5, 0.1875),
        "gain_mid": jnp.clip(1.0 + 0.18 * jax.random.normal(seeds[5], (W2,), jnp.float32), 0.1, 1.9),
        "qkv_mid": draw_qkv_mid(jax.random.fold_in(seeds[12], 71), 0),
        "out_mid": scatter_about(seeds[7], (W2, W2), W2 ** -0.5, 0.25),
        "merge_mid": scatter_about(seeds[8], (4 * W2, W3), (4 * W2) ** -0.5, 0.125),
        "gain_coarse": jnp.clip(1.0 + 0.18 * jax.random.normal(seeds[9], (W3,), jnp.float32), 0.1, 1.9),
        "qkv_coarse": draw_qkv_coarse(jax.random.fold_in(seeds[12], 71), 0),
        "out_coarse": scatter_about(seeds[11], (W3, W3), W3 ** -0.5, 0.1875),
    }


EPSILON = 1e-06
REACH = 3
NEG_FILL = -1e+30

def rms_norm(values, gains):
    wide = values.astype(jnp.float32)
    factor = lax.rsqrt(lax.optimization_barrier(jnp.mean(wide * wide, axis=-1, keepdims=True)) + EPSILON)
    return (wide * factor * gains.astype(jnp.float32)).astype(jnp.bfloat16)

def project(values, weight):
    flattened = values.reshape(-1, values.shape[-1])
    result = jnp.dot(flattened, weight, preferred_element_type=jnp.float32)
    return result.reshape(values.shape[:-1] + (weight.shape[1],))

def merge_blocks(values, weight):
    height, breadth, channels = values.shape
    grouped = values.reshape(height // 2, 2, breadth // 2, 2, channels).transpose(0, 2, 1, 3, 4)
    grouped = grouped.reshape(height // 2, breadth // 2, 4 * channels)
    return project(grouped, weight).astype(jnp.bfloat16)

def neighbour_attention(queries, padded, row_first, col_first, all_rows, all_cols):
    height, breadth, channels = queries.shape
    head_count = channels // HEAD
    factor = HEAD ** (-0.5)
    query_heads = queries.reshape(height, breadth, head_count, HEAD).astype(jnp.float32)
    row_place = row_first + jnp.arange(height, dtype=jnp.int32)
    col_place = col_first + jnp.arange(breadth, dtype=jnp.int32)
    score_list = []
    for shift_y in range(2 * REACH + 1):
        row_key = row_place + shift_y - REACH
        row_inside = (row_key >= 0) & (row_key < all_rows)
        for shift_x in range(2 * REACH + 1):
            col_key = col_place + shift_x - REACH
            col_inside = (col_key >= 0) & (col_key < all_cols)
            inside = row_inside[:, None, None] & col_inside[None, :, None]
            key_rows = padded[shift_y:shift_y + height, shift_x:shift_x + breadth, :channels]
            key_heads = key_rows.reshape(height, breadth, head_count, HEAD).astype(jnp.float32)
            scores = jnp.einsum('rchd,rchd->rch', query_heads, key_heads) * factor
            score_list.append(jnp.where(inside, scores, NEG_FILL))
    stacked = jnp.stack(score_list, axis=-1)
    row_max = lax.optimization_barrier(jnp.max(stacked, axis=-1, keepdims=True))
    weights = jnp.exp(stacked - row_max)
    denominator = lax.optimization_barrier(jnp.sum(weights, axis=-1))
    rounded = weights.astype(jnp.bfloat16)
    accumulated = jnp.zeros((height, breadth, head_count, HEAD), jnp.float32)
    offset = 0
    for shift_y in range(2 * REACH + 1):
        for shift_x in range(2 * REACH + 1):
            value_rows = padded[shift_y:shift_y + height, shift_x:shift_x + breadth, channels:]
            value_heads = value_rows.reshape(height, breadth, head_count, HEAD).astype(jnp.float32)
            accumulated = accumulated + rounded[..., offset:offset + 1].astype(jnp.float32) * value_heads
            offset += 1
    result = accumulated / denominator[..., None]
    return result.reshape(height, breadth, channels).astype(jnp.bfloat16)

def fine_level(values, gains, w_qkv, w_out, w_merge):
    height, breadth, channels = values.shape
    normed = rms_norm(values, gains)
    projected = project(normed, w_qkv).astype(jnp.bfloat16)
    padded = jnp.pad(projected[..., channels:], ((REACH, REACH), (REACH, REACH), (0, 0)))
    attended = neighbour_attention(projected[..., :channels], padded, 0, 0, height, breadth)
    result = (values.astype(jnp.float32) + project(attended, w_out)).astype(jnp.bfloat16)
    return (result, merge_blocks(result, w_merge))

def coarse_level(values, gains, w_qkv, w_out):
    height, breadth, channels = values.shape
    tok_count = height * breadth
    flattened = values.reshape(tok_count, channels)
    normed = rms_norm(flattened, gains)
    projected = project(normed, w_qkv).astype(jnp.bfloat16)
    head_count = channels // HEAD
    sections = projected.reshape(tok_count, 3, head_count, HEAD).transpose(1, 2, 0, 3)
    block_size = math.gcd(tok_count, 2048)
    factor = HEAD ** (-0.5)

    def per_head(triple):
        queries, key_rows, value_rows = triple

        def per_block(query_block):
            scores = jnp.dot(query_block, key_rows.T, preferred_element_type=jnp.float32) * factor
            row_max = lax.optimization_barrier(jnp.max(scores, axis=-1, keepdims=True))
            weights = jnp.exp(scores - row_max)
            denominator = lax.optimization_barrier(jnp.sum(weights, axis=-1, keepdims=True))
            accumulated = jnp.dot(weights.astype(jnp.bfloat16), value_rows, preferred_element_type=jnp.float32)
            return (accumulated / denominator).astype(jnp.bfloat16)
        blocks = queries.reshape(tok_count // block_size, block_size, HEAD)
        return lax.map(per_block, blocks).reshape(tok_count, HEAD)
    attended = lax.map(per_head, (sections[0], sections[1], sections[2]))
    attended = attended.transpose(1, 0, 2).reshape(tok_count, channels)
    result = (flattened.astype(jnp.float32) + project(attended, w_out)).astype(jnp.bfloat16)
    return result.reshape(height, breadth, channels)

def reference(image, gain_fine, qkv_fine, out_fine, merge_fine, gain_mid, qkv_mid, out_mid, merge_mid, gain_coarse, qkv_coarse, out_coarse):
    skip_fine, merged_fine = fine_level(image, gain_fine, qkv_fine, out_fine, merge_fine)
    skip_mid, merged_mid = fine_level(merged_fine, gain_mid, qkv_mid, out_mid, merge_mid)
    coarse_out = coarse_level(merged_mid, gain_coarse, qkv_coarse, out_coarse)
    return (skip_fine, skip_mid, coarse_out)
```

```python
import functools

import jax
import jax.numpy as jnp
from jax import lax
from jax.experimental import pallas as pl
from jax.experimental.pallas import tpu as pltpu
from jax.sharding import PartitionSpec as P

MESH = pl.DeviceIdType.MESH
HEAD = 64
REACH = 3
EPSILON = 1e-06
NEG_FILL = -1e30
GROUP = 256
STRIP = 128
CORES = 2
SPLIT = 2
F32 = jnp.float32
BF16 = jnp.bfloat16


def iota(shape, dim):
    return lax.broadcasted_iota(jnp.int32, shape, dim)


def rms_norm(values, gains):
    wide = values.astype(F32)
    factor = lax.rsqrt(jnp.mean(wide * wide, axis=-1, keepdims=True) + EPSILON)
    return (wide * factor * gains).astype(BF16)


def dot(left, right):
    return jnp.dot(left, right, preferred_element_type=F32)


def dot_t(left, right):
    return lax.dot_general(left, right, (((1,), (1,)), ((), ())), preferred_element_type=F32)


def strip_places(slot, height, breadth):
    side = slot < 8 * height
    second = slot >= 4 * height
    across = slot & 3
    corner = slot - 8 * height
    down = corner >= 32
    along = (corner >> 2) & 3
    last = (side & second) | (~side & ((corner & 16) != 0))
    col = across + jnp.where(last, breadth - 3, 0)
    row = jnp.where(
        side,
        (slot - jnp.where(second, 4 * height, 0)) >> 2,
        along + jnp.where(down, height - 3, 0),
    )
    valid = (across < 3) & (side | ((along < 3) & (corner < 64)))
    key_col = col + jnp.where(last, -breadth, breadth)
    key_row = row + jnp.where(side, 0, jnp.where(down, -height, height))
    return row, col, key_row, key_col, valid


def pack_strip(block, height, breadth):
    tokens = height * breadth
    row, col, _, _, valid = strip_places(iota((STRIP, 1), 0), height, breadth)
    token = jnp.where(valid, row * breadth + col, -1)
    pick = jnp.where(token == iota((STRIP, tokens), 1), 1.0, 0.0).astype(BF16)
    return dot(pick, block).astype(BF16)


def merge_blocks(block, weight_ref, height, breadth):
    tokens, channels = block.shape
    merged = tokens // 4
    place = iota((tokens, 1), 0)
    part = place // merged
    index = place % merged
    half = breadth // 2
    token = (2 * (index // half) + part // 2) * breadth + 2 * (index % half) + part % 2
    pick = jnp.where(token == iota((tokens, tokens), 1), 1.0, 0.0).astype(BF16)
    grouped = dot(pick, block).astype(BF16)
    total = None
    for p in range(4):
        term = dot(
            grouped[p * merged : (p + 1) * merged], weight_ref[p * channels : (p + 1) * channels, :]
        )
        total = term if total is None else total + term
    return total.astype(BF16)


def halo_copies(src, own, packed, halo, strip, sends, recvs, height, breadth, here, grid):
    row, col = here
    rows, cols = grid
    up, down = lax.rem(row + rows - 1, rows), lax.rem(row + 1, rows)
    left, right = lax.rem(col + cols - 1, cols), lax.rem(col + 1, cols)
    wide = 3 * breadth
    tall = 4 * height
    corner = 8 * height

    def copy(k, source, target, device):
        return pltpu.make_async_remote_copy(
            src_ref=source,
            dst_ref=target,
            send_sem=sends.at[k],
            recv_sem=recvs.at[k],
            device_id=device,
            device_id_type=MESH,
        )

    tokens = height * breadth
    straight = [
        copy(
            0,
            src.at[pl.ds(own, wide)],
            halo.at[pl.ds((height + 3) * breadth, wide)],
            (up, col),
        ),
        copy(
            1,
            src.at[pl.ds(own + tokens - wide, wide)],
            halo.at[pl.ds(0, wide)],
            (down, col),
        ),
    ]
    around = []
    spans = [
        (0, tall, (row, left)),
        (tall, tall, (row, right)),
        (corner, 16, (up, left)),
        (corner + 16, 16, (up, right)),
        (corner + 32, 16, (down, left)),
        (corner + 48, 16, (down, right)),
    ]
    for k, (first, count, device) in enumerate(spans):
        around.append(
            copy(2 + k, packed.at[pl.ds(first, count)], strip.at[pl.ds(first, count)], device)
        )
    return straight, around


def project_own(block, gain, weight_ref, q_ref, kv_ref, height, breadth):
    channels = block.shape[1]
    projected = dot(rms_norm(block, gain), weight_ref[...])
    q_ref[...] = (projected[:, :channels] * HEAD ** (-0.5)).astype(BF16)
    kv_ref[pl.ds(3 * breadth, height * breadth)] = projected[:, channels:].astype(BF16)


def project_halo(halo, strip, gain, weight_ref, kv_ref, kvs_ref, height, breadth):
    channels = halo.shape[1]
    wide = 3 * breadth
    weight = weight_ref[:, channels:]
    for first in (0, (height + 3) * breadth):
        part = dot(rms_norm(halo[pl.ds(first, wide)], gain), weight)
        kv_ref[pl.ds(first, wide)] = part.astype(BF16)
    kvs_ref[...] = dot(rms_norm(strip[...], gain), weight).astype(BF16)


def center_bias(breadth):
    queries, keys = 2 * breadth, 8 * breadth
    q = iota((queries, 1), 0)
    k = iota((1, keys), 1)
    row_gap = k // breadth - q // breadth
    col_gap = k % breadth - q % breadth
    near = (row_gap >= 0) & (row_gap <= 2 * REACH) & (jnp.abs(col_gap) <= REACH)
    return jnp.where(near, 0.0, NEG_FILL)


def neighbour_attention(
    q_ref, kv_ref, kvs_ref, bias_ref, att_ref, channels, height, breadth, here, grid
):
    row, col = here
    rows, cols = grid
    heads = GROUP // HEAD
    queries, keys = 2 * breadth, 8 * breadth
    groups = channels // GROUP
    first_row, first_col = row * height, col * breadth
    bias_ref[...] = center_bias(breadth)
    lane_head = iota((1, GROUP), 1) // HEAD
    marks = [jnp.where(lane_head == h, 1.0, 0.0) for h in range(heads)]
    _, _, key_row, key_col, valid = strip_places(iota((1, STRIP), 1), height, breadth)
    inside = (
        valid
        & (first_row + key_row >= 0)
        & (first_row + key_row < rows * height)
        & (first_col + key_col >= 0)
        & (first_col + key_col < cols * breadth)
    )
    q_place = iota((queries, 1), 0)
    strip_near = inside & (jnp.abs(key_col - q_place % breadth) <= REACH)
    row_gap = key_row - q_place // breadth
    key_place = iota((1, keys), 1) // breadth - REACH + first_row

    def step(i, carry):
        first = pl.multiple_of(i * queries, queries)
        place = key_place + 2 * i
        row_bias = jnp.where((place >= 0) & (place < rows * height), 0.0, NEG_FILL)
        bias = bias_ref[...] + row_bias
        gap = row_gap - 2 * i
        strip_bias = jnp.where(strip_near & (gap >= -REACH) & (gap <= REACH), 0.0, NEG_FILL)
        for g in range(groups):
            lanes = slice(g * GROUP, (g + 1) * GROUP)
            v_lanes = slice(channels + g * GROUP, channels + (g + 1) * GROUP)
            q = q_ref[pl.ds(first, queries), lanes]
            stacked = jnp.concatenate([q * m.astype(BF16) for m in marks], axis=0)
            center = dot_t(stacked, kv_ref[pl.ds(first, keys), lanes])
            edge = dot_t(stacked, kvs_ref[:, lanes])
            center = center.reshape(heads, queries, keys) + bias[None]
            edge = edge.reshape(heads, queries, STRIP) + strip_bias[None]
            top = jnp.maximum(
                jnp.max(center, axis=-1, keepdims=True), jnp.max(edge, axis=-1, keepdims=True)
            )
            center = jnp.exp(center - top)
            edge = jnp.exp(edge - top)
            total = jnp.sum(center, axis=-1, keepdims=True) + jnp.sum(edge, axis=-1, keepdims=True)
            out = dot(
                center.astype(BF16).reshape(heads * queries, keys),
                kv_ref[pl.ds(first, keys), v_lanes],
            ) + dot(edge.astype(BF16).reshape(heads * queries, STRIP), kvs_ref[:, v_lanes])
            out = out.reshape(heads, queries, GROUP) / total
            picked = out[0] * marks[0]
            for h in range(1, heads):
                picked = picked + out[h] * marks[h]
            att_ref[pl.ds(first, queries), lanes] = picked.astype(BF16)
        return carry

    lax.fori_loop(0, height // 2, step, 0)


def kernel(
    sizes,
    image,
    g1,
    qkv1,
    out1,
    merge1,
    g2,
    qkv2,
    out2,
    merge2,
    g3,
    qkv3,
    out3,
    skip1,
    skip2,
    last,
    w_qkv1,
    w_out1,
    w_merge1,
    w_qkv2,
    w_out2,
    w_merge2,
    w_qkv3,
    w_out3,
    x1,
    pack1,
    strip1,
    q1,
    kv1,
    kvs1,
    att1,
    res1,
    bias1,
    x2,
    pack2,
    strip2,
    q2,
    kv2,
    kvs2,
    att2,
    res2,
    bias2,
    x3,
    head_out,
    head_in,
    kv_all,
    top,
    total,
    acc,
    back_out,
    back_in,
    att3,
    res3,
    load_sem,
    save_sem,
    halo1_send,
    halo1_recv,
    halo2_send,
    halo2_recv,
    head_send,
    head_recv,
    ring_send,
    pair_send,
    kv_recv,
    back_send,
    back_recv,
):
    h1, c1, h2, c2, t3, rows, cols = sizes
    grid = (rows, cols)
    row, col = lax.axis_index("row"), lax.axis_index("col")
    here = (row, col)
    members = rows // CORES * SPLIT
    around = cols // SPLIT
    core = lax.rem(row, CORES)
    base = row - core
    part = lax.rem(col, SPLIT)
    turn = col // SPLIT
    mine = (row // CORES) * SPLIT + part

    def member(g):
        return ((g // SPLIT) * CORES + core, turn * SPLIT + lax.rem(g, SPLIT))

    def on_ring(y):
        return (row, y * SPLIT + part)

    other = (base + (CORES - 1) - core, col)

    loads = [
        pltpu.make_async_copy(src, dst, load_sem.at[k])
        for k, (src, dst) in enumerate(
            [
                (image, x1.at[pl.ds(3 * c1, h1 * c1)]),
                (qkv1, w_qkv1),
                (out1, w_out1),
                (merge1, w_merge1),
                (qkv2, w_qkv2),
                (out2, w_out2),
                (merge2, w_merge2),
                (qkv3, w_qkv3),
                (out3, w_out3),
            ]
        )
    ]
    for load in loads:
        load.start()

    barrier = pltpu.get_barrier_semaphore()

    def greet(device):
        pl.semaphore_signal(barrier, inc=1, device_id=device, device_id_type=MESH)

    for down in (rows - 1, 0, 1):
        for right in (cols - 1, 0, 1):
            if down or right:
                greet((lax.rem(row + down, rows), lax.rem(col + right, cols)))
    for j in range(1, members):
        greet(member(lax.rem(mine + j, members)))
    for j in range(1, around):
        greet(on_ring(lax.rem(turn + j, around)))
    greet(other)

    strip2[pl.ds(8 * h2 + 64, STRIP - 8 * h2 - 64)] = jnp.zeros(
        (STRIP - 8 * h2 - 64, strip2.shape[1]), BF16
    )
    straight, edges = halo_copies(
        image, 0, pack1, x1, strip1, halo1_send, halo1_recv, h1, c1, here, grid
    )
    loads[0].wait()
    block = x1[pl.ds(3 * c1, h1 * c1)]
    pack1[...] = pack_strip(block, h1, c1)
    pl.semaphore_wait(barrier, 8 + members - 1 + around - 1 + 1)
    for copy in straight + edges:
        copy.start()
    loads[1].wait()
    project_own(block, g1[...], w_qkv1, q1, kv1, h1, c1)
    for copy in straight + edges:
        copy.wait_recv()
    project_halo(x1, strip1, g1[...], w_qkv1, kv1, kvs1, h1, c1)
    neighbour_attention(q1, kv1, kvs1, bias1, att1, x1.shape[1], h1, c1, here, grid)
    loads[2].wait()
    res1[...] = (
        x1[pl.ds(3 * c1, h1 * c1)].astype(F32) + dot(att1[...], w_out1[...])
    ).astype(BF16)
    save1 = pltpu.make_async_copy(res1, skip1, save_sem.at[0])
    save1.start()
    loads[3].wait()
    block = merge_blocks(res1[...], w_merge1, h1, c1)

    x2[pl.ds(3 * c2, h2 * c2)] = block
    straight2, edges2 = halo_copies(
        x2, 3 * c2, pack2, x2, strip2, halo2_send, halo2_recv, h2, c2, here, grid
    )
    for copy in straight2:
        copy.start()
    pack2[...] = pack_strip(block, h2, c2)
    for copy in edges2:
        copy.start()
    loads[4].wait()
    project_own(block, g2[...], w_qkv2, q2, kv2, h2, c2)
    for copy in straight2 + edges2:
        copy.wait_recv()
    project_halo(x2, strip2, g2[...], w_qkv2, kv2, kvs2, h2, c2)
    neighbour_attention(q2, kv2, kvs2, bias2, att2, x2.shape[1], h2, c2, here, grid)
    loads[5].wait()
    res2[...] = (
        x2[pl.ds(3 * c2, h2 * c2)].astype(F32) + dot(att2[...], w_out2[...])
    ).astype(BF16)
    save2 = pltpu.make_async_copy(res2, skip2, save_sem.at[1])
    save2.start()
    loads[6].wait()
    block = merge_blocks(res2[...], w_merge2, h2, c2)
    x3[...] = block

    channels = x3.shape[1]
    loads[7].wait()
    projected = dot(rms_norm(block, g3[...]), w_qkv3[...])
    low = iota((1, 2 * HEAD), 1) < HEAD
    for pair in range(channels // (2 * HEAD)):
        tiles = [
            projected[:, s * channels + pair * 128 : s * channels + (pair + 1) * 128]
            for s in range(3)
        ]
        turned = [pltpu.roll(tile, HEAD, 1) for tile in tiles]
        scale = HEAD ** (-0.5)
        head_out[2 * pair, 0:t3] = jnp.where(low, tiles[0] * scale, 0.0).astype(BF16)
        head_out[2 * pair, t3:] = jnp.where(low, tiles[1], turned[2]).astype(BF16)
        head_out[2 * pair + 1, 0:t3] = jnp.where(low, turned[0] * scale, 0.0).astype(BF16)
        head_out[2 * pair + 1, t3:] = jnp.where(low, turned[1], tiles[2]).astype(BF16)

    def head_copy(j):
        g = lax.rem(mine + j, members)
        return pltpu.make_async_remote_copy(
            src_ref=head_out.at[g],
            dst_ref=head_in.at[mine],
            send_sem=head_send.at[g],
            recv_sem=head_recv.at[mine],
            device_id=member(g),
            device_id_type=MESH,
        )

    def head_arrival(j):
        g = lax.rem(mine + j, members)
        return pltpu.make_async_remote_copy(
            src_ref=head_out.at[g],
            dst_ref=head_in.at[g],
            send_sem=head_send.at[g],
            recv_sem=head_recv.at[g],
            device_id=member(g),
            device_id_type=MESH,
        )

    for j in range(1, members):
        head_copy(j).start()
    head_in[mine] = head_out[mine]
    for j in range(1, members):
        head_arrival(j).wait_recv()

    slot = turn * CORES + core
    count = members * t3
    kv_all[slot] = head_in[:, t3:, :].reshape(count, 128)

    def ring_copy(j):
        return pltpu.make_async_remote_copy(
            src_ref=kv_all.at[slot],
            dst_ref=kv_all.at[slot],
            send_sem=ring_send.at[j],
            recv_sem=kv_recv.at[slot],
            device_id=on_ring(lax.rem(turn + j, around)),
            device_id_type=MESH,
        )

    def pair_copy(j, place):
        return pltpu.make_async_remote_copy(
            src_ref=kv_all.at[place],
            dst_ref=kv_all.at[place],
            send_sem=pair_send.at[j],
            recv_sem=kv_recv.at[place],
            device_id=other,
            device_id_type=MESH,
        )

    order = [j for j in (0, 1, 3, 2) if j < around]
    for j in order[1:]:
        ring_copy(j).start()
    top[...] = jnp.full(top.shape, NEG_FILL, F32)
    total[...] = jnp.zeros(total.shape, F32)
    acc[...] = jnp.zeros(acc.shape, F32)

    def absorb(place):
        queries = head_in[:, 0:t3, :].reshape(count, 128)
        block = kv_all[place]
        score = dot_t(queries, block)
        before = top[...]
        now = jnp.maximum(before, jnp.max(score, axis=-1, keepdims=True))
        ratio = jnp.exp(before - now)
        weight = jnp.exp(score - now)
        top[...] = now
        total[...] = total[...] * ratio + jnp.sum(weight, axis=-1, keepdims=True)
        acc[...] = acc[...] * ratio + dot(weight.astype(BF16), block)

    for j in order:
        y = lax.rem(turn + j, around)
        near, far = y * CORES + core, y * CORES + (CORES - 1) - core
        if j:
            pair_copy(j, near).wait_recv()
        pair_copy(j, near).start()
        absorb(near)
        pair_copy(j, far).wait_recv()
        absorb(far)

    back_out[...] = (acc[...] / total[...]).astype(BF16).reshape(members, t3, 128)

    def back_copy(j):
        g = lax.rem(mine + j, members)
        return pltpu.make_async_remote_copy(
            src_ref=back_out.at[g],
            dst_ref=back_in.at[mine],
            send_sem=back_send.at[g],
            recv_sem=back_recv.at[mine],
            device_id=member(g),
            device_id_type=MESH,
        )

    def back_arrival(j):
        g = lax.rem(mine + j, members)
        return pltpu.make_async_remote_copy(
            src_ref=back_out.at[g],
            dst_ref=back_in.at[g],
            send_sem=back_send.at[g],
            recv_sem=back_recv.at[g],
            device_id=member(g),
            device_id_type=MESH,
        )

    for j in range(1, members):
        back_copy(j).start()
    back_in[mine] = back_out[mine]
    for j in range(1, members):
        back_arrival(j).wait_recv()
    for pair in range(channels // (2 * HEAD)):
        even = pltpu.roll(back_in[2 * pair].astype(F32), HEAD, 1)
        odd = back_in[2 * pair + 1].astype(F32)
        att3[:, pair * 128 : (pair + 1) * 128] = jnp.where(low, even, odd).astype(BF16)
    loads[8].wait()
    res3[...] = (x3[...].astype(F32) + dot(att3[...], w_out3[...])).astype(BF16)
    save3 = pltpu.make_async_copy(res3, last, save_sem.at[2])
    save3.start()

    for copy in straight + edges + straight2 + edges2:
        copy.wait_send()
    for j in range(1, members):
        head_copy(j).wait_send()
        back_copy(j).wait_send()
    for j in order:
        if j:
            ring_copy(j).wait_send()
        y = lax.rem(turn + j, around)
        pair_copy(j, y * CORES + core).wait_send()
    save1.wait()
    save2.wait()
    save3.wait()


def shards(
    rows,
    cols,
    image,
    gain_fine,
    qkv_fine,
    out_fine,
    merge_fine,
    gain_mid,
    qkv_mid,
    out_mid,
    merge_mid,
    gain_coarse,
    qkv_coarse,
    out_coarse,
):
    h1, c1, w1 = image.shape
    w2, w3 = gain_mid.shape[0], gain_coarse.shape[0]
    h2, c2 = h1 // 2, c1 // 2
    h3, c3 = h2 // 2, c2 // 2
    t1, t2, t3 = h1 * c1, h2 * c2, h3 * c3
    members = rows // CORES * SPLIT
    around = cols // SPLIT
    sizes = (h1, c1, h2, c2, t3, rows, cols)
    anywhere = pl.BlockSpec(memory_space=pl.ANY)
    local = pl.BlockSpec(memory_space=pltpu.VMEM)

    def vmem(*shape):
        return pltpu.VMEM(shape, BF16)

    def level(height, breadth, width):
        tokens, reach = height * breadth, (height + 6) * breadth
        return [
            vmem(reach, width),
            vmem(STRIP, width),
            vmem(STRIP, width),
            vmem(tokens, width),
            vmem(reach, 2 * width),
            vmem(STRIP, 2 * width),
            vmem(tokens, width),
            vmem(tokens, width),
            pltpu.VMEM((2 * breadth, 8 * breadth), F32),
        ]

    def dma(*shape):
        return pltpu.SemaphoreType.DMA(shape)

    count = members * t3
    scratch = (
        [vmem(*w.shape) for w in (qkv_fine, out_fine, merge_fine, qkv_mid, out_mid, merge_mid)]
        + [vmem(*w.shape) for w in (qkv_coarse, out_coarse)]
        + level(h1, c1, w1)
        + level(h2, c2, w2)
        + [
            vmem(t3, w3),
            vmem(members, 2 * t3, 128),
            vmem(members, 2 * t3, 128),
            vmem(CORES * around, count, 128),
            pltpu.VMEM((count, 1), F32),
            pltpu.VMEM((count, 1), F32),
            pltpu.VMEM((count, 128), F32),
            vmem(members, t3, 128),
            vmem(members, t3, 128),
            vmem(t3, w3),
            vmem(t3, w3),
        ]
        + [dma(9), dma(3), dma(8), dma(8), dma(8), dma(8)]
        + [dma(members), dma(members), dma(around), dma(around), dma(CORES * around)]
        + [dma(members), dma(members)]
    )
    skip_fine, skip_mid, coarse_out = pl.pallas_call(
        functools.partial(kernel, sizes),
        out_shape=(
            jax.ShapeDtypeStruct((t1, w1), BF16),
            jax.ShapeDtypeStruct((t2, w2), BF16),
            jax.ShapeDtypeStruct((t3, w3), BF16),
        ),
        in_specs=[
            anywhere,
            local,
            anywhere,
            anywhere,
            anywhere,
            local,
            anywhere,
            anywhere,
            anywhere,
            local,
            anywhere,
            anywhere,
        ],
        out_specs=(anywhere, anywhere, anywhere),
        scratch_shapes=scratch,
        compiler_params=pltpu.CompilerParams(
            collective_id=0, has_side_effects=True, vmem_limit_bytes=52 * 1024 * 1024
        ),
    )(
        image.reshape(t1, w1),
        gain_fine.reshape(1, w1),
        qkv_fine,
        out_fine,
        merge_fine,
        gain_mid.reshape(1, w2),
        qkv_mid,
        out_mid,
        merge_mid,
        gain_coarse.reshape(1, w3),
        qkv_coarse,
        out_coarse,
    )
    return (
        skip_fine.reshape(h1, c1, w1),
        skip_mid.reshape(h2, c2, w2),
        coarse_out.reshape(h3, c3, w3),
    )


def solution(mesh):
    placed = (P("row", "col", None),) + (P(),) * 11
    rows, cols = mesh.shape["row"], mesh.shape["col"]
    return jax.shard_map(
        functools.partial(shards, rows, cols),
        mesh=mesh,
        in_specs=placed,
        out_specs=(P("row", "col", None),) * 3,
        check_vma=False,
    )
```

```python
import functools

import jax
import jax.numpy as jnp
from jax import lax
from jax.experimental import pallas as pl
from jax.experimental.pallas import tpu as pltpu
from jax.sharding import PartitionSpec as P

MESH = pl.DeviceIdType.MESH
HEAD = 64
REACH = 3
EPSILON = 1e-06
NEG_FILL = -1e30
GROUP = 256
STRIP = 128
CORES = 2
SPLIT = 2
F32 = jnp.float32
BF16 = jnp.bfloat16


def iota(shape, dim):
    return lax.broadcasted_iota(jnp.int32, shape, dim)


def rms_norm(values, gains):
    wide = values.astype(F32)
    factor = lax.rsqrt(jnp.mean(wide * wide, axis=-1, keepdims=True) + EPSILON)
    return (wide * factor * gains).astype(BF16)


def dot(left, right):
    return jnp.dot(left, right, preferred_element_type=F32)


def dot_t(left, right):
    return lax.dot_general(left, right, (((1,), (1,)), ((), ())), preferred_element_type=F32)


def strip_places(slot, height, breadth):
    side = slot < 8 * height
    second = slot >= 4 * height
    across = slot & 3
    corner = slot - 8 * height
    down = corner >= 32
    along = (corner >> 2) & 3
    last = (side & second) | (~side & ((corner & 16) != 0))
    col = across + jnp.where(last, breadth - 3, 0)
    row = jnp.where(
        side,
        (slot - jnp.where(second, 4 * height, 0)) >> 2,
        along + jnp.where(down, height - 3, 0),
    )
    valid = (across < 3) & (side | ((along < 3) & (corner < 64)))
    key_col = col + jnp.where(last, -breadth, breadth)
    key_row = row + jnp.where(side, 0, jnp.where(down, -height, height))
    return row, col, key_row, key_col, valid


def pack_strip(block, height, breadth):
    tokens = height * breadth
    row, col, _, _, valid = strip_places(iota((STRIP, 1), 0), height, breadth)
    token = jnp.where(valid, row * breadth + col, -1)
    pick = jnp.where(token == iota((STRIP, tokens), 1), 1.0, 0.0).astype(BF16)
    return dot(pick, block).astype(BF16)


def merge_blocks(block, weight_ref, height, breadth):
    tokens, channels = block.shape
    merged = tokens // 4
    place = iota((tokens, 1), 0)
    part = place // merged
    index = place % merged
    half = breadth // 2
    token = (2 * (index // half) + part // 2) * breadth + 2 * (index % half) + part % 2
    pick = jnp.where(token == iota((tokens, tokens), 1), 1.0, 0.0).astype(BF16)
    grouped = dot(pick, block).astype(BF16)
    total = None
    for p in range(4):
        term = dot(
            grouped[p * merged : (p + 1) * merged], weight_ref[p * channels : (p + 1) * channels, :]
        )
        total = term if total is None else total + term
    return total.astype(BF16)


def halo_copies(
    src, own, packed, halo, above, below, strip, sends, recvs, height, breadth, here, grid
):
    row, col = here
    rows, cols = grid
    up, down = lax.rem(row + rows - 1, rows), lax.rem(row + 1, rows)
    left, right = lax.rem(col + cols - 1, cols), lax.rem(col + 1, cols)
    wide = 3 * breadth
    tall = 4 * height
    corner = 8 * height

    def copy(k, source, target, device):
        return pltpu.make_async_remote_copy(
            src_ref=source,
            dst_ref=target,
            send_sem=sends.at[k],
            recv_sem=recvs.at[k],
            device_id=device,
            device_id_type=MESH,
        )

    tokens = height * breadth
    straight = [
        copy(
            0,
            src.at[pl.ds(own, wide)],
            halo.at[pl.ds(below, wide)],
            (up, col),
        ),
        copy(
            1,
            src.at[pl.ds(own + tokens - wide, wide)],
            halo.at[pl.ds(above, wide)],
            (down, col),
        ),
    ]
    around = []
    spans = [
        (0, tall, (row, left)),
        (tall, tall, (row, right)),
        (corner, 16, (up, left)),
        (corner + 16, 16, (up, right)),
        (corner + 32, 16, (down, left)),
        (corner + 48, 16, (down, right)),
    ]
    for k, (first, count, device) in enumerate(spans):
        around.append(
            copy(
                2 + k,
                packed.at[pl.ds(first, count)],
                halo.at[pl.ds(strip + first, count)],
                device,
            )
        )
    return straight, around


def transposed(values):
    return values.astype(F32).T.astype(BF16)


def soften(parts):
    top = jnp.max(parts[0], axis=0, keepdims=True)
    for part in parts[1:]:
        top = jnp.maximum(top, jnp.max(part, axis=0, keepdims=True))
    weights = [jnp.exp(part - top) for part in parts]
    total = jnp.sum(weights[0], axis=0, keepdims=True)
    for weight in weights[1:]:
        total = total + jnp.sum(weight, axis=0, keepdims=True)
    return [weight.astype(BF16) for weight in weights], 1.0 / total


def stack_heads(queries):
    lane_head = iota((1, GROUP), 1) // HEAD
    return jnp.concatenate(
        [queries * jnp.where(lane_head == h, 1.0, 0.0).astype(BF16) for h in range(GROUP // HEAD)],
        axis=0,
    )


def head_values(terms, inverse, count):
    blocks = []
    for pair in range(GROUP // HEAD // 2):
        rows = slice(pair * 2 * HEAD, (pair + 1) * 2 * HEAD)
        lanes = slice(pair * 2 * count, (pair + 1) * 2 * count)
        both = None
        for values, weights in terms:
            term = dot(values[rows], weights[:, lanes])
            both = term if both is None else both + term
        both = both * inverse[:, lanes]
        blocks += [both[:HEAD, :count], both[HEAD:, count:]]
    return jnp.concatenate(blocks, axis=0).T.astype(BF16)


def inside_grid(key_row, key_col, height, breadth, here, grid):
    first_row, first_col = here[0] * height, here[1] * breadth
    return (
        (first_row + key_row >= 0)
        & (first_row + key_row < grid[0] * height)
        & (first_col + key_col >= 0)
        & (first_col + key_col < grid[1] * breadth)
    )


def fine_attention(q_ref, k_ref, vt_ref, bias_ref, att_ref, height, breadth, here, grid):
    heads = GROUP // HEAD
    queries, keys = 2 * breadth, 8 * breadth
    edge = (height + 6) * breadth
    _, _, strip_row, strip_col, valid = strip_places(iota((STRIP, 1), 0), height, breadth)
    strip_inside = valid & inside_grid(strip_row, strip_col, height, breadth, here, grid)
    query = iota((1, queries), 1)
    strip_near = strip_inside & (jnp.abs(strip_col - query % breadth) <= REACH)
    row_gap = strip_row - query // breadth
    key_place = iota((keys, 1), 0) // breadth - REACH + here[0] * height

    def step(i, carry):
        first = pl.multiple_of(i * queries, queries)
        place = key_place + 2 * i
        row_bias = jnp.where((place >= 0) & (place < grid[0] * height), 0.0, NEG_FILL)
        bias = bias_ref[...] + row_bias
        gap = row_gap - 2 * i
        strip_bias = jnp.where(strip_near & (gap >= -REACH) & (gap <= REACH), 0.0, NEG_FILL)
        stacked = stack_heads(q_ref[pl.ds(first, queries), :])
        center = dot_t(k_ref[pl.ds(first, keys), :], stacked)
        center = center + jnp.concatenate([bias] * heads, axis=1)
        strip = dot_t(k_ref[pl.ds(edge, STRIP), :], stacked)
        strip = strip + jnp.concatenate([strip_bias] * heads, axis=1)
        (center, strip), inverse = soften([center, strip])
        terms = [
            (vt_ref[:, pl.ds(first, keys)], center),
            (vt_ref[:, edge : edge + STRIP], strip),
        ]
        att_ref[pl.ds(first, queries), :] = head_values(terms, inverse, queries)
        return carry

    lax.fori_loop(0, height // 2, step, 0)


def fine_bias(breadth):
    keys, queries = 8 * breadth, 2 * breadth
    k = iota((keys, queries), 0)
    q = iota((keys, queries), 1)
    row_gap = k // breadth - q // breadth
    col_gap = k % breadth - q % breadth
    near = (row_gap >= 0) & (row_gap <= 2 * REACH) & (jnp.abs(col_gap) <= REACH)
    return jnp.where(near, 0.0, NEG_FILL)


def mid_bias(height, breadth, here, grid):
    block = height * breadth
    wide = 3 * breadth
    k = iota((4 * block, 1), 0)
    part = k // block
    index = k % block
    row, col = index // breadth, index % breadth
    _, _, strip_row, strip_col, strip_valid = strip_places(index, height, breadth)
    is_strip = part == 3
    shift = jnp.where(part == 1, -REACH, jnp.where(part == 2, height, 0))
    key_row = jnp.where(is_strip, strip_row, row + shift)
    key_col = jnp.where(is_strip, strip_col, col)
    valid = (is_strip & strip_valid) | ((part == 0) | (~is_strip & (index < wide)))
    valid = valid & inside_grid(key_row, key_col, height, breadth, here, grid)
    q = iota((1, block), 1)
    near = (jnp.abs(key_row - q // breadth) <= REACH) & (jnp.abs(key_col - q % breadth) <= REACH)
    return jnp.where(valid & near, 0.0, NEG_FILL)


def mid_attention(q_ref, k_ref, vt_ref, bias_ref, att_ref):
    count, channels = q_ref.shape
    heads = GROUP // HEAD
    for g in range(channels // GROUP):
        lanes = slice(g * GROUP, (g + 1) * GROUP)
        score = dot_t(k_ref[:, lanes], stack_heads(q_ref[:, lanes]))
        score = score + jnp.concatenate([bias_ref[...]] * heads, axis=1)
        (weight,), inverse = soften([score])
        att_ref[:, lanes] = head_values([(vt_ref[lanes, :], weight)], inverse, count)


def kernel(
    sizes,
    image,
    gain1,
    qkv1,
    out1,
    merge1,
    gain2,
    qkv2,
    out2,
    merge2,
    gain3,
    qkv3,
    out3,
    skip1,
    skip2,
    last,
    w_qkv1,
    w_out1,
    w_merge1,
    w_qkv2,
    w_out2,
    w_merge2,
    w_qkv3,
    w_out3,
    g1,
    g2,
    g3,
    x1,
    pack1,
    turned1,
    q1,
    k1,
    vt1,
    att1,
    res1,
    bias1,
    x2,
    pack2,
    turned2,
    q2,
    k2,
    vt2,
    att2,
    res2,
    bias2,
    x3,
    head_out,
    head_in,
    kv_all,
    top,
    total,
    acc,
    back_out,
    back_in,
    att3,
    res3,
    load_sem,
    save_sem,
    halo1_send,
    halo1_recv,
    halo2_send,
    halo2_recv,
    head_send,
    head_recv,
    plane_send,
    pair_send,
    kv_recv,
    back_send,
    back_recv,
    plane_sem,
):
    h1, c1, h2, c2, t3, rows, cols = sizes
    grid = (rows, cols)
    row, col = lax.axis_index("row"), lax.axis_index("col")
    here = (row, col)
    members = rows // CORES * SPLIT
    around = cols // SPLIT
    core = lax.rem(row, CORES)
    base = row - core
    part = lax.rem(col, SPLIT)
    turn = col // SPLIT
    mine = (row // CORES) * SPLIT + part

    def member(g):
        return ((g // SPLIT) * CORES + core, turn * SPLIT + lax.rem(g, SPLIT))

    def on_ring(y):
        return (row, y * SPLIT + part)

    other = (base + (CORES - 1) - core, col)

    loads = [
        pltpu.make_async_copy(src, dst, load_sem.at[k])
        for k, (src, dst) in enumerate(
            [
                (image, x1.at[pl.ds(3 * c1, h1 * c1)]),
                (qkv1, w_qkv1),
                (out1, w_out1),
                (merge1, w_merge1),
                (qkv2, w_qkv2),
                (out2, w_out2),
                (merge2, w_merge2),
                (qkv3, w_qkv3),
                (out3, w_out3),
                (gain1, g1),
                (gain2, g2),
                (gain3, g3),
            ]
        )
    ]
    early = (0, 1, 9)
    for k in early:
        loads[k].start()

    barrier = pltpu.get_barrier_semaphore()

    def greet(device):
        pl.semaphore_signal(barrier, inc=1, device_id=device, device_id_type=MESH)

    for down in (rows - 1, 0, 1):
        for right in (cols - 1, 0, 1):
            if down or right:
                greet((lax.rem(row + down, rows), lax.rem(col + right, cols)))
    for j in range(1, members):
        greet(member(lax.rem(mine + j, members)))
    for j in range(1, around):
        greet(on_ring(lax.rem(turn + j, around)))
    greet(other)

    n1, n2 = h1 * c1, h2 * c2
    w1, w2 = x1.shape[1], x2.shape[1]
    own1, below1, edge1 = 3 * c1, (h1 + 3) * c1, (h1 + 6) * c1
    straight, edges = halo_copies(
        image, 0, pack1, x1, 0, below1, edge1, halo1_send, halo1_recv, h1, c1, here, grid
    )
    pl.semaphore_wait(barrier, 8 + members - 1 + around - 1 + 1)
    for j in range(1, around):
        pl.semaphore_signal(
            plane_sem, inc=1, device_id=on_ring(lax.rem(turn + j, around)), device_id_type=MESH
        )
    for copy in straight:
        copy.start()
    loads[0].wait()
    block = x1[pl.ds(own1, n1)]
    pack1[...] = pack_strip(block, h1, c1)
    for copy in edges:
        copy.start()
    for k, load in enumerate(loads):
        if k not in early:
            load.start()
    loads[9].wait()
    loads[1].wait()
    turned1[...] = transposed(w_qkv1[:, 2 * w1 :])
    normed = rms_norm(block, g1[...])
    projected = dot(normed, w_qkv1[:, : 2 * w1])
    q1[...] = (projected[:, :w1] * HEAD ** (-0.5)).astype(BF16)
    k1[pl.ds(own1, n1)] = projected[:, w1:].astype(BF16)
    vt1[:, own1:below1] = dot_t(turned1[...], normed).astype(BF16)
    bias1[...] = fine_bias(c1)
    for first in (n2 + 3 * c2, 2 * n2 + 3 * c2):
        x2[pl.ds(first, n2 - 3 * c2)] = jnp.zeros((n2 - 3 * c2, w2), BF16)
    used = 3 * n2 + 8 * h2 + 64
    x2[pl.ds(used, 4 * n2 - used)] = jnp.zeros((4 * n2 - used, w2), BF16)
    for copy in straight + edges:
        copy.wait_recv()
    for first, count in ((0, 3 * c1), (below1, 3 * c1), (edge1, STRIP)):
        normed = rms_norm(x1[pl.ds(first, count)], g1[...])
        k1[pl.ds(first, count)] = dot(normed, w_qkv1[:, w1 : 2 * w1]).astype(BF16)
        vt1[:, first : first + count] = dot_t(turned1[...], normed).astype(BF16)
    fine_attention(q1, k1, vt1, bias1, att1, h1, c1, here, grid)
    loads[2].wait()
    res1[...] = (x1[pl.ds(own1, n1)].astype(F32) + dot(att1[...], w_out1[...])).astype(BF16)
    save1 = pltpu.make_async_copy(res1, skip1, save_sem.at[0])
    save1.start()
    loads[3].wait()
    block = merge_blocks(res1[...], w_merge1, h1, c1)

    x2[pl.ds(0, n2)] = block
    straight2, edges2 = halo_copies(
        x2, 0, pack2, x2, n2, 2 * n2, 3 * n2, halo2_send, halo2_recv, h2, c2, here, grid
    )
    for copy in straight2:
        copy.start()
    pack2[...] = pack_strip(block, h2, c2)
    for copy in edges2:
        copy.start()
    loads[10].wait()
    loads[4].wait()
    turned2[...] = transposed(w_qkv2[:, 2 * w2 :])
    bias2[...] = mid_bias(h2, c2, here, grid)
    normed = rms_norm(block, g2[...])
    projected = dot(normed, w_qkv2[:, : 2 * w2])
    q2[...] = (projected[:, :w2] * HEAD ** (-0.5)).astype(BF16)
    k2[pl.ds(0, n2)] = projected[:, w2:].astype(BF16)
    vt2[:, :n2] = dot_t(turned2[...], normed).astype(BF16)
    for copy in straight2 + edges2:
        copy.wait_recv()
    normed = rms_norm(x2[pl.ds(n2, 3 * n2)], g2[...])
    k2[pl.ds(n2, 3 * n2)] = dot(normed, w_qkv2[:, w2 : 2 * w2]).astype(BF16)
    vt2[:, n2:] = dot_t(turned2[...], normed).astype(BF16)
    mid_attention(q2, k2, vt2, bias2, att2)
    loads[5].wait()
    res2[...] = (block.astype(F32) + dot(att2[...], w_out2[...])).astype(BF16)
    save2 = pltpu.make_async_copy(res2, skip2, save_sem.at[1])
    save2.start()
    loads[6].wait()
    block = merge_blocks(res2[...], w_merge2, h2, c2)
    x3[...] = block

    channels = x3.shape[1]
    loads[11].wait()
    loads[7].wait()
    projected = dot(rms_norm(block, g3[...]), w_qkv3[...])
    low = iota((1, 2 * HEAD), 1) < HEAD
    for pair in range(channels // (2 * HEAD)):
        tiles = [
            projected[:, s * channels + pair * 128 : s * channels + (pair + 1) * 128]
            for s in range(3)
        ]
        turned = [pltpu.roll(tile, HEAD, 1) for tile in tiles]
        scale = HEAD ** (-0.5)
        head_out[2 * pair, 0:t3] = jnp.where(low, tiles[0] * scale, 0.0).astype(BF16)
        head_out[2 * pair, t3:] = jnp.where(low, tiles[1], turned[2]).astype(BF16)
        head_out[2 * pair + 1, 0:t3] = jnp.where(low, turned[0] * scale, 0.0).astype(BF16)
        head_out[2 * pair + 1, t3:] = jnp.where(low, turned[1], tiles[2]).astype(BF16)

    def head_copy(j):
        g = lax.rem(mine + j, members)
        return pltpu.make_async_remote_copy(
            src_ref=head_out.at[g],
            dst_ref=head_in.at[mine],
            send_sem=head_send.at[g],
            recv_sem=head_recv.at[mine],
            device_id=member(g),
            device_id_type=MESH,
        )

    def head_arrival(j):
        g = lax.rem(mine + j, members)
        return pltpu.make_async_remote_copy(
            src_ref=head_out.at[g],
            dst_ref=head_in.at[g],
            send_sem=head_send.at[g],
            recv_sem=head_recv.at[g],
            device_id=member(g),
            device_id_type=MESH,
        )

    slot = turn * CORES + core
    count = members * t3
    order = [j for j in (0, 1, 3, 2) if j < around]

    def plane_copy(j, g):
        y = lax.rem(turn + j, around)
        return pltpu.make_async_remote_copy(
            src_ref=head_out.at[g, pl.ds(t3, t3)],
            dst_ref=kv_all.at[slot, mine],
            send_sem=plane_send.at[j],
            recv_sem=kv_recv.at[slot],
            device_id=((g // SPLIT) * CORES + core, y * SPLIT + lax.rem(g, SPLIT)),
            device_id_type=MESH,
        )

    def pair_copy(j, place):
        return pltpu.make_async_remote_copy(
            src_ref=kv_all.at[place],
            dst_ref=kv_all.at[place],
            send_sem=pair_send.at[j],
            recv_sem=kv_recv.at[place],
            device_id=other,
            device_id_type=MESH,
        )

    def plane_sent(j):
        return pltpu.make_async_remote_copy(
            src_ref=kv_all.at[slot],
            dst_ref=kv_all.at[slot],
            send_sem=plane_send.at[j],
            recv_sem=kv_recv.at[slot],
            device_id=on_ring(lax.rem(turn + j, around)),
            device_id_type=MESH,
        )

    for j in range(1, members):
        head_copy(j).start()
    pl.semaphore_wait(plane_sem, around - 1)
    for j in order[1:]:
        for g in range(members):
            plane_copy(j, lax.rem(mine + g, members)).start()
    head_in[mine] = head_out[mine]
    top[...] = jnp.full(top.shape, NEG_FILL, F32)
    total[...] = jnp.zeros(total.shape, F32)
    acc[...] = jnp.zeros(acc.shape, F32)
    for j in range(1, members):
        head_arrival(j).wait_recv()
    kv_all[slot] = head_in[:, t3:, :]

    queries = head_in[:, 0:t3, :].reshape(count, 128)
    pick = jnp.where(iota((HEAD, 128), 0) + HEAD == iota((HEAD, 128), 1), 1.0, 0.0).astype(BF16)

    def absorb(places):
        blocks = [kv_all[place].reshape(count, 128) for place in places]
        scores = [dot_t(block, queries) for block in blocks]
        before = top[...]
        now = before
        for score in scores:
            now = jnp.maximum(now, jnp.max(score, axis=0, keepdims=True))
        ratio = jnp.exp(before - now)
        top[...] = now
        part, update = total[...] * ratio, acc[...] * ratio
        for score, block in zip(scores, blocks):
            weight = jnp.exp(score - now)
            part = part + jnp.sum(weight, axis=0, keepdims=True)
            update = update + dot(dot_t(pick, block).astype(BF16), weight.astype(BF16))
        total[...] = part
        acc[...] = update

    waiting = []
    for j in order:
        y = lax.rem(turn + j, around)
        near, far = y * CORES + core, y * CORES + (CORES - 1) - core
        if j:
            pair_copy(j, near).wait_recv()
        pair_copy(j, near).start()
        if waiting:
            pair_copy(j, waiting[0]).wait_recv()
        absorb(waiting + [near])
        waiting = [far]
    pair_copy(0, waiting[0]).wait_recv()
    absorb(waiting)

    result = acc[...] * (1.0 / total[...])
    result = jnp.concatenate([result, result], axis=0).T
    back_out[...] = result.astype(BF16).reshape(members, t3, 128)

    def back_copy(j):
        g = lax.rem(mine + j, members)
        return pltpu.make_async_remote_copy(
            src_ref=back_out.at[g],
            dst_ref=back_in.at[mine],
            send_sem=back_send.at[g],
            recv_sem=back_recv.at[mine],
            device_id=member(g),
            device_id_type=MESH,
        )

    def back_arrival(j):
        g = lax.rem(mine + j, members)
        return pltpu.make_async_remote_copy(
            src_ref=back_out.at[g],
            dst_ref=back_in.at[g],
            send_sem=back_send.at[g],
            recv_sem=back_recv.at[g],
            device_id=member(g),
            device_id_type=MESH,
        )

    for j in range(1, members):
        back_copy(j).start()
    back_in[mine] = back_out[mine]
    for j in range(1, members):
        back_arrival(j).wait_recv()
    for pair in range(channels // (2 * HEAD)):
        even, odd = back_in[2 * pair].astype(F32), back_in[2 * pair + 1].astype(F32)
        att3[:, pair * 128 : (pair + 1) * 128] = jnp.where(low, even, odd).astype(BF16)
    loads[8].wait()
    res3[...] = (x3[...].astype(F32) + dot(att3[...], w_out3[...])).astype(BF16)
    save3 = pltpu.make_async_copy(res3, last, save_sem.at[2])
    save3.start()

    for copy in straight + edges + straight2 + edges2:
        copy.wait_send()
    for j in range(1, members):
        head_copy(j).wait_send()
        back_copy(j).wait_send()
    for j in order:
        if j:
            plane_sent(j).wait_send()
        y = lax.rem(turn + j, around)
        pair_copy(j, y * CORES + core).wait_send()
    save1.wait()
    save2.wait()
    save3.wait()


def shards(
    rows,
    cols,
    image,
    gain_fine,
    qkv_fine,
    out_fine,
    merge_fine,
    gain_mid,
    qkv_mid,
    out_mid,
    merge_mid,
    gain_coarse,
    qkv_coarse,
    out_coarse,
):
    h1, c1, w1 = image.shape
    w2, w3 = gain_mid.shape[0], gain_coarse.shape[0]
    h2, c2 = h1 // 2, c1 // 2
    h3, c3 = h2 // 2, c2 // 2
    t1, t2, t3 = h1 * c1, h2 * c2, h3 * c3
    members = rows // CORES * SPLIT
    around = cols // SPLIT
    sizes = (h1, c1, h2, c2, t3, rows, cols)
    anywhere = pl.BlockSpec(memory_space=pl.ANY)

    def vmem(*shape):
        return pltpu.VMEM(shape, BF16)

    def level(tokens, width, keys, bias):
        return [
            vmem(keys, width),
            vmem(STRIP, width),
            vmem(width, width),
            vmem(tokens, width),
            vmem(keys, width),
            vmem(width, keys),
            vmem(tokens, width),
            vmem(tokens, width),
            pltpu.VMEM(bias, F32),
        ]

    def dma(*shape):
        return pltpu.SemaphoreType.DMA(shape)

    count = members * t3
    scratch = (
        [vmem(*w.shape) for w in (qkv_fine, out_fine, merge_fine, qkv_mid, out_mid, merge_mid)]
        + [vmem(*w.shape) for w in (qkv_coarse, out_coarse)]
        + [pltpu.VMEM((1, w), F32) for w in (w1, w2, w3)]
        + level(t1, w1, (h1 + 6) * c1 + STRIP, (8 * c1, 2 * c1))
        + level(t2, w2, 4 * t2, (4 * t2, t2))
        + [
            vmem(t3, w3),
            vmem(members, 2 * t3, 128),
            vmem(members, 2 * t3, 128),
            vmem(CORES * around, members, t3, 128),
            pltpu.VMEM((1, count), F32),
            pltpu.VMEM((1, count), F32),
            pltpu.VMEM((HEAD, count), F32),
            vmem(members, t3, 128),
            vmem(members, t3, 128),
            vmem(t3, w3),
            vmem(t3, w3),
        ]
        + [dma(12), dma(3), dma(8), dma(8), dma(8), dma(8)]
        + [dma(members), dma(members), dma(around), dma(around), dma(CORES * around)]
        + [dma(members), dma(members), pltpu.SemaphoreType.REGULAR]
    )
    skip_fine, skip_mid, coarse_out = pl.pallas_call(
        functools.partial(kernel, sizes),
        out_shape=(
            jax.ShapeDtypeStruct((t1, w1), BF16),
            jax.ShapeDtypeStruct((t2, w2), BF16),
            jax.ShapeDtypeStruct((t3, w3), BF16),
        ),
        in_specs=[anywhere] * 12,
        out_specs=(anywhere, anywhere, anywhere),
        scratch_shapes=scratch,
        compiler_params=pltpu.CompilerParams(
            collective_id=0, has_side_effects=True, vmem_limit_bytes=60 * 1024 * 1024
        ),
    )(
        image.reshape(t1, w1),
        gain_fine.reshape(1, w1),
        qkv_fine,
        out_fine,
        merge_fine,
        gain_mid.reshape(1, w2),
        qkv_mid,
        out_mid,
        merge_mid,
        gain_coarse.reshape(1, w3),
        qkv_coarse,
        out_coarse,
    )
    return (
        skip_fine.reshape(h1, c1, w1),
        skip_mid.reshape(h2, c2, w2),
        coarse_out.reshape(h3, c3, w3),
    )


def solution(mesh):
    placed = (P("row", "col", None),) + (P(),) * 11
    rows, cols = mesh.shape["row"], mesh.shape["col"]
    return jax.shard_map(
        functools.partial(shards, rows, cols),
        mesh=mesh,
        in_specs=placed,
        out_specs=(P("row", "col", None),) * 3,
        check_vma=False,
    )
```

```python
import functools

import jax
import jax.numpy as jnp
from jax import lax
from jax.experimental import pallas as pl
from jax.experimental.pallas import tpu as pltpu
from jax.sharding import PartitionSpec as P

MESH = pl.DeviceIdType.MESH
HEAD = 64
REACH = 3
EPSILON = 1e-06
NEG_FILL = -1e30
GROUP = 256
STRIP = 128
CORES = 2
SIDE = 4
FAR = ((0, 0, 0), (2, 2, 0), (2, 0, 2), (0, 2, 2))
NEAR = (
    (0, 0, 0),
    (1, 1, 1),
    (3, 3, 3),
    (0, 2, 0),
    (3, 3, 0),
    (3, 1, 0),
    (1, 0, 1),
    (1, 0, 3),
    (0, 3, 3),
    (0, 3, 1),
    (1, 0, 0),
    (3, 0, 0),
    (0, 1, 0),
    (0, 3, 0),
    (0, 0, 1),
    (0, 0, 3),
)
F32 = jnp.float32
BF16 = jnp.bfloat16


def iota(shape, dim):
    return lax.broadcasted_iota(jnp.int32, shape, dim)


def rms_norm(values, gains):
    wide = values.astype(F32)
    factor = lax.rsqrt(jnp.mean(wide * wide, axis=-1, keepdims=True) + EPSILON)
    return (wide * factor * gains).astype(BF16)


def dot(left, right):
    return jnp.dot(left, right, preferred_element_type=F32)


def dot_t(left, right):
    return lax.dot_general(left, right, (((1,), (1,)), ((), ())), preferred_element_type=F32)


def strip_places(slot, height, breadth):
    side = slot < 8 * height
    second = slot >= 4 * height
    across = slot & 3
    corner = slot - 8 * height
    down = corner >= 32
    along = (corner >> 2) & 3
    last = (side & second) | (~side & ((corner & 16) != 0))
    col = across + jnp.where(last, breadth - 3, 0)
    row = jnp.where(
        side,
        (slot - jnp.where(second, 4 * height, 0)) >> 2,
        along + jnp.where(down, height - 3, 0),
    )
    valid = (across < 3) & (side | ((along < 3) & (corner < 64)))
    key_col = col + jnp.where(last, -breadth, breadth)
    key_row = row + jnp.where(side, 0, jnp.where(down, -height, height))
    return row, col, key_row, key_col, valid


def pack_strip(block, height, breadth):
    tokens = height * breadth
    row, col, _, _, valid = strip_places(iota((STRIP, 1), 0), height, breadth)
    token = jnp.where(valid, row * breadth + col, -1)
    pick = jnp.where(token == iota((STRIP, tokens), 1), 1.0, 0.0).astype(BF16)
    return dot(pick, block).astype(BF16)


def merge_blocks(block, weight_ref, height, breadth):
    tokens, channels = block.shape
    merged = tokens // 4
    place = iota((tokens, 1), 0)
    part = place // merged
    index = place % merged
    half = breadth // 2
    token = (2 * (index // half) + part // 2) * breadth + 2 * (index % half) + part % 2
    pick = jnp.where(token == iota((tokens, tokens), 1), 1.0, 0.0).astype(BF16)
    grouped = dot(pick, block).astype(BF16)
    total = None
    for p in range(4):
        term = dot(
            grouped[p * merged : (p + 1) * merged], weight_ref[p * channels : (p + 1) * channels, :]
        )
        total = term if total is None else total + term
    return total.astype(BF16)


def halo_copies(
    src, own, packed, halo, above, below, strip, sends, recvs, height, breadth, here, grid
):
    row, col = here
    rows, cols = grid
    up, down = lax.rem(row + rows - 1, rows), lax.rem(row + 1, rows)
    left, right = lax.rem(col + cols - 1, cols), lax.rem(col + 1, cols)
    wide = 3 * breadth
    tall = 4 * height
    corner = 8 * height

    def copy(k, source, target, device):
        return pltpu.make_async_remote_copy(
            src_ref=source,
            dst_ref=target,
            send_sem=sends.at[k],
            recv_sem=recvs.at[k],
            device_id=device,
            device_id_type=MESH,
        )

    tokens = height * breadth
    straight = [
        copy(
            0,
            src.at[pl.ds(own, wide)],
            halo.at[pl.ds(below, wide)],
            (up, col),
        ),
        copy(
            1,
            src.at[pl.ds(own + tokens - wide, wide)],
            halo.at[pl.ds(above, wide)],
            (down, col),
        ),
    ]
    around = []
    spans = [
        (0, tall, (row, left)),
        (tall, tall, (row, right)),
        (corner, 16, (up, left)),
        (corner + 16, 16, (up, right)),
        (corner + 32, 16, (down, left)),
        (corner + 48, 16, (down, right)),
    ]
    for k, (first, count, device) in enumerate(spans):
        around.append(
            copy(
                2 + k,
                packed.at[pl.ds(first, count)],
                halo.at[pl.ds(strip + first, count)],
                device,
            )
        )
    return straight, around


def transposed(values):
    return values.astype(F32).T.astype(BF16)


def soften(parts):
    top = jnp.max(parts[0], axis=0, keepdims=True)
    for part in parts[1:]:
        top = jnp.maximum(top, jnp.max(part, axis=0, keepdims=True))
    weights = [jnp.exp(part - top) for part in parts]
    total = jnp.sum(weights[0], axis=0, keepdims=True)
    for weight in weights[1:]:
        total = total + jnp.sum(weight, axis=0, keepdims=True)
    return [weight.astype(BF16) for weight in weights], 1.0 / total


def stack_heads(queries):
    lane_head = iota((1, GROUP), 1) // HEAD
    return jnp.concatenate(
        [queries * jnp.where(lane_head == h, 1.0, 0.0).astype(BF16) for h in range(GROUP // HEAD)],
        axis=0,
    )


def head_values(terms, inverse, count):
    blocks = []
    for pair in range(GROUP // HEAD // 2):
        rows = slice(pair * 2 * HEAD, (pair + 1) * 2 * HEAD)
        lanes = slice(pair * 2 * count, (pair + 1) * 2 * count)
        both = None
        for values, weights in terms:
            term = dot(values[rows], weights[:, lanes])
            both = term if both is None else both + term
        both = both * inverse[:, lanes]
        blocks += [both[:HEAD, :count], both[HEAD:, count:]]
    return jnp.concatenate(blocks, axis=0).T.astype(BF16)


def inside_grid(key_row, key_col, height, breadth, here, grid):
    first_row, first_col = here[0] * height, here[1] * breadth
    return (
        (first_row + key_row >= 0)
        & (first_row + key_row < grid[0] * height)
        & (first_col + key_col >= 0)
        & (first_col + key_col < grid[1] * breadth)
    )


def fine_attention(q_ref, k_ref, vt_ref, bias_ref, att_ref, height, breadth, here, grid):
    heads = GROUP // HEAD
    queries, keys = 2 * breadth, 8 * breadth
    edge = (height + 6) * breadth
    _, _, strip_row, strip_col, valid = strip_places(iota((STRIP, 1), 0), height, breadth)
    strip_inside = valid & inside_grid(strip_row, strip_col, height, breadth, here, grid)
    query = iota((1, queries), 1)
    strip_near = strip_inside & (jnp.abs(strip_col - query % breadth) <= REACH)
    row_gap = strip_row - query // breadth
    key_place = iota((keys, 1), 0) // breadth - REACH + here[0] * height

    def step(i, carry):
        first = pl.multiple_of(i * queries, queries)
        place = key_place + 2 * i
        row_bias = jnp.where((place >= 0) & (place < grid[0] * height), 0.0, NEG_FILL)
        bias = bias_ref[...] + row_bias
        gap = row_gap - 2 * i
        strip_bias = jnp.where(strip_near & (gap >= -REACH) & (gap <= REACH), 0.0, NEG_FILL)
        stacked = stack_heads(q_ref[pl.ds(first, queries), :])
        center = dot_t(k_ref[pl.ds(first, keys), :], stacked)
        center = center + jnp.concatenate([bias] * heads, axis=1)
        strip = dot_t(k_ref[pl.ds(edge, STRIP), :], stacked)
        strip = strip + jnp.concatenate([strip_bias] * heads, axis=1)
        (center, strip), inverse = soften([center, strip])
        terms = [
            (vt_ref[:, pl.ds(first, keys)], center),
            (vt_ref[:, edge : edge + STRIP], strip),
        ]
        att_ref[pl.ds(first, queries), :] = head_values(terms, inverse, queries)
        return carry

    lax.fori_loop(0, height // 2, step, 0)


def fine_bias(breadth):
    keys, queries = 8 * breadth, 2 * breadth
    k = iota((keys, queries), 0)
    q = iota((keys, queries), 1)
    row_gap = k // breadth - q // breadth
    col_gap = k % breadth - q % breadth
    near = (row_gap >= 0) & (row_gap <= 2 * REACH) & (jnp.abs(col_gap) <= REACH)
    return jnp.where(near, 0.0, NEG_FILL)


def mid_bias(height, breadth, here, grid):
    block = height * breadth
    wide = 3 * breadth
    k = iota((4 * block, 1), 0)
    part = k // block
    index = k % block
    row, col = index // breadth, index % breadth
    _, _, strip_row, strip_col, strip_valid = strip_places(index, height, breadth)
    is_strip = part == 3
    shift = jnp.where(part == 1, -REACH, jnp.where(part == 2, height, 0))
    key_row = jnp.where(is_strip, strip_row, row + shift)
    key_col = jnp.where(is_strip, strip_col, col)
    valid = (is_strip & strip_valid) | ((part == 0) | (~is_strip & (index < wide)))
    valid = valid & inside_grid(key_row, key_col, height, breadth, here, grid)
    q = iota((1, block), 1)
    near = (jnp.abs(key_row - q // breadth) <= REACH) & (jnp.abs(key_col - q % breadth) <= REACH)
    return jnp.where(valid & near, 0.0, NEG_FILL)


def mid_attention(q_ref, k_ref, vt_ref, bias_ref, att_ref):
    count, channels = q_ref.shape
    heads = GROUP // HEAD
    for g in range(channels // GROUP):
        lanes = slice(g * GROUP, (g + 1) * GROUP)
        score = dot_t(k_ref[:, lanes], stack_heads(q_ref[:, lanes]))
        score = score + jnp.concatenate([bias_ref[...]] * heads, axis=1)
        (weight,), inverse = soften([score])
        att_ref[:, lanes] = head_values([(vt_ref[lanes, :], weight)], inverse, count)


def kernel(
    sizes,
    image,
    gain1,
    qkv1,
    out1,
    merge1,
    gain2,
    qkv2,
    out2,
    merge2,
    gain3,
    qkv3,
    out3,
    skip1,
    skip2,
    last,
    w_qkv1,
    w_out1,
    w_merge1,
    w_qkv2,
    w_out2,
    w_merge2,
    w_qkv3,
    w_out3,
    g1,
    g2,
    g3,
    x1,
    pack1,
    turned1,
    q1,
    k1,
    vt1,
    att1,
    bias1,
    x2,
    pack2,
    turned2,
    q2,
    k2,
    vt2,
    att2,
    bias2,
    x3,
    head_out,
    head_in,
    kv_all,
    top,
    total,
    acc,
    back_out,
    back_in,
    att3,
    load_sem,
    halo1_send,
    halo1_recv,
    halo2_send,
    halo2_recv,
    head_send,
    head_recv,
    far_send,
    pair_send,
    kv_recv,
    back_send,
    back_recv,
    plane_sem,
):
    h1, c1, h2, c2, t3, rows, cols = sizes
    grid = (rows, cols)
    row, col = lax.axis_index("row"), lax.axis_index("col")
    here = (row, col)
    members, around = len(NEAR), len(FAR)
    core = lax.rem(row, CORES)
    spot = (
        lax.rem(row // CORES, SIDE),
        col // 2,
        lax.rem(col, 2) * 2 + row // (CORES * SIDE),
    )

    def chip(*shifts):
        return tuple(
            lax.rem(spot[d] + sum(shift[d] for shift in shifts) % SIDE, SIDE) for d in range(3)
        )

    def device(place):
        x, y, z = place
        return (lax.rem(z, 2) * (SIDE * CORES) + x * CORES + core, y * 2 + z // 2)

    def head_of(place):
        x, y, z = place
        high = lax.rem(x // 2 + y // 2 + z // 2, 2)
        return lax.rem(x, 2) + 2 * lax.rem(y, 2) + 4 * lax.rem(z, 2) + 8 * high

    def back_along(shift):
        return tuple(-step % SIDE for step in shift)

    mine = head_of(spot)
    other = (row - core + (CORES - 1) - core, col)

    loads = [
        pltpu.make_async_copy(src, dst, load_sem.at[k])
        for k, (src, dst) in enumerate(
            [
                (image, x1.at[pl.ds(3 * c1, h1 * c1)]),
                (qkv1, w_qkv1),
                (out1, w_out1),
                (merge1, w_merge1),
                (qkv2, w_qkv2),
                (out2, w_out2),
                (merge2, w_merge2),
                (qkv3, w_qkv3),
                (out3, w_out3),
                (gain1, g1),
                (gain2, g2),
                (gain3, g3),
            ]
        )
    ]
    early = (0, 1, 9)
    for k in early:
        loads[k].start()

    barrier = pltpu.get_barrier_semaphore()

    def greet(device):
        pl.semaphore_signal(barrier, inc=1, device_id=device, device_id_type=MESH)

    for down in (rows - 1, 0, 1):
        for right in (cols - 1, 0, 1):
            if down or right:
                greet((lax.rem(row + down, rows), lax.rem(col + right, cols)))
    around_here = sorted({shift for near in NEAR[1:] for shift in (near, back_along(near))})
    for shift in around_here + list(FAR[1:]):
        greet(device(chip(shift)))
    greet(other)

    n1, n2 = h1 * c1, h2 * c2
    w1, w2 = x1.shape[1], x2.shape[1]
    own1, below1, edge1 = 3 * c1, (h1 + 3) * c1, (h1 + 6) * c1
    straight, edges = halo_copies(
        image, 0, pack1, x1, 0, below1, edge1, halo1_send, halo1_recv, h1, c1, here, grid
    )
    pl.semaphore_wait(barrier, 8 + len(around_here) + around - 1 + 1)
    for far in FAR[1:]:
        pl.semaphore_signal(plane_sem, inc=1, device_id=device(chip(far)), device_id_type=MESH)
    for copy in straight:
        copy.start()
    loads[0].wait()
    block = x1[pl.ds(own1, n1)]
    pack1[...] = pack_strip(block, h1, c1)
    for copy in edges:
        copy.start()
    for k, load in enumerate(loads):
        if k not in early:
            load.start()
    loads[9].wait()
    loads[1].wait()
    turned1[...] = transposed(w_qkv1[:, 2 * w1 :])
    normed = rms_norm(block, g1[...])
    projected = dot(normed, w_qkv1[:, : 2 * w1])
    q1[...] = (projected[:, :w1] * HEAD ** (-0.5)).astype(BF16)
    k1[pl.ds(own1, n1)] = projected[:, w1:].astype(BF16)
    vt1[:, own1:below1] = dot_t(turned1[...], normed).astype(BF16)
    bias1[...] = fine_bias(c1)
    for first in (n2 + 3 * c2, 2 * n2 + 3 * c2):
        x2[pl.ds(first, n2 - 3 * c2)] = jnp.zeros((n2 - 3 * c2, w2), BF16)
    used = 3 * n2 + 8 * h2 + 64
    x2[pl.ds(used, 4 * n2 - used)] = jnp.zeros((4 * n2 - used, w2), BF16)
    for copy in straight + edges:
        copy.wait_recv()
    for first, count in ((0, 3 * c1), (below1, 3 * c1), (edge1, STRIP)):
        normed = rms_norm(x1[pl.ds(first, count)], g1[...])
        k1[pl.ds(first, count)] = dot(normed, w_qkv1[:, w1 : 2 * w1]).astype(BF16)
        vt1[:, first : first + count] = dot_t(turned1[...], normed).astype(BF16)
    fine_attention(q1, k1, vt1, bias1, att1, h1, c1, here, grid)
    loads[2].wait()
    skip1[...] = (x1[pl.ds(own1, n1)].astype(F32) + dot(att1[...], w_out1[...])).astype(BF16)
    loads[3].wait()
    block = merge_blocks(skip1[...], w_merge1, h1, c1)

    x2[pl.ds(0, n2)] = block
    straight2, edges2 = halo_copies(
        x2, 0, pack2, x2, n2, 2 * n2, 3 * n2, halo2_send, halo2_recv, h2, c2, here, grid
    )
    for copy in straight2:
        copy.start()
    pack2[...] = pack_strip(block, h2, c2)
    for copy in edges2:
        copy.start()
    loads[10].wait()
    loads[4].wait()
    turned2[...] = transposed(w_qkv2[:, 2 * w2 :])
    bias2[...] = mid_bias(h2, c2, here, grid)
    normed = rms_norm(block, g2[...])
    projected = dot(normed, w_qkv2[:, : 2 * w2])
    q2[...] = (projected[:, :w2] * HEAD ** (-0.5)).astype(BF16)
    k2[pl.ds(0, n2)] = projected[:, w2:].astype(BF16)
    vt2[:, :n2] = dot_t(turned2[...], normed).astype(BF16)
    for copy in straight2 + edges2:
        copy.wait_recv()
    normed = rms_norm(x2[pl.ds(n2, 3 * n2)], g2[...])
    k2[pl.ds(n2, 3 * n2)] = dot(normed, w_qkv2[:, w2 : 2 * w2]).astype(BF16)
    vt2[:, n2:] = dot_t(turned2[...], normed).astype(BF16)
    mid_attention(q2, k2, vt2, bias2, att2)
    loads[5].wait()
    skip2[...] = (block.astype(F32) + dot(att2[...], w_out2[...])).astype(BF16)
    loads[6].wait()
    block = merge_blocks(skip2[...], w_merge2, h2, c2)
    x3[...] = block

    channels = x3.shape[1]
    loads[11].wait()
    loads[7].wait()
    projected = dot(rms_norm(block, g3[...]), w_qkv3[...])
    low = iota((1, 2 * HEAD), 1) < HEAD
    for pair in range(channels // (2 * HEAD)):
        tiles = [
            projected[:, s * channels + pair * 128 : s * channels + (pair + 1) * 128]
            for s in range(3)
        ]
        turned = [pltpu.roll(tile, HEAD, 1) for tile in tiles]
        scale = HEAD ** (-0.5)
        head_out[2 * pair, 0:t3] = jnp.where(low, tiles[0] * scale, 0.0).astype(BF16)
        head_out[2 * pair, t3:] = jnp.where(low, tiles[1], turned[2]).astype(BF16)
        head_out[2 * pair + 1, 0:t3] = jnp.where(low, turned[0] * scale, 0.0).astype(BF16)
        head_out[2 * pair + 1, t3:] = jnp.where(low, turned[1], tiles[2]).astype(BF16)

    def head_copy(j):
        place = chip(NEAR[j])
        return pltpu.make_async_remote_copy(
            src_ref=head_out.at[head_of(place)],
            dst_ref=head_in.at[j],
            send_sem=head_send.at[j],
            recv_sem=head_recv.at[j],
            device_id=device(place),
            device_id_type=MESH,
        )

    count = members * t3

    def far_copy(f, j):
        place = chip(NEAR[j], FAR[f])
        return pltpu.make_async_remote_copy(
            src_ref=head_out.at[head_of(place), pl.ds(t3, t3)],
            dst_ref=kv_all.at[f * CORES + core, j],
            send_sem=far_send.at[f],
            recv_sem=kv_recv.at[f * CORES + core],
            device_id=device(place),
            device_id_type=MESH,
        )

    def pair_copy(f):
        return pltpu.make_async_remote_copy(
            src_ref=kv_all.at[f * CORES + core],
            dst_ref=kv_all.at[f * CORES + core],
            send_sem=pair_send.at[f],
            recv_sem=kv_recv.at[f * CORES + core],
            device_id=other,
            device_id_type=MESH,
        )

    def arrival(place):
        return pltpu.make_async_remote_copy(
            src_ref=kv_all.at[place],
            dst_ref=kv_all.at[place],
            send_sem=pair_send.at[0],
            recv_sem=kv_recv.at[place],
            device_id=other,
            device_id_type=MESH,
        )

    def far_sent(f):
        return pltpu.make_async_remote_copy(
            src_ref=kv_all.at[core],
            dst_ref=kv_all.at[core],
            send_sem=far_send.at[f],
            recv_sem=kv_recv.at[core],
            device_id=other,
            device_id_type=MESH,
        )

    for j in range(1, members):
        head_copy(j).start()
    pl.semaphore_wait(plane_sem, around - 1)
    for f in range(1, around):
        for j in range(members):
            far_copy(f, j).start()
    head_in[0] = head_out[mine]
    top[...] = jnp.full(top.shape, NEG_FILL, F32)
    total[...] = jnp.zeros(total.shape, F32)
    acc[...] = jnp.zeros(acc.shape, F32)
    for j in range(1, members):
        head_copy(j).wait_recv()
    kv_all[core] = head_in[:, t3:, :]

    queries = head_in[:, 0:t3, :].reshape(count, 128)
    pick = jnp.where(iota((HEAD, 128), 0) + HEAD == iota((HEAD, 128), 1), 1.0, 0.0).astype(BF16)

    def absorb(places):
        blocks = [kv_all[place].reshape(count, 128) for place in places]
        scores = [dot_t(block, queries) for block in blocks]
        before = top[...]
        now = before
        for score in scores:
            now = jnp.maximum(now, jnp.max(score, axis=0, keepdims=True))
        ratio = jnp.exp(before - now)
        top[...] = now
        part, update = total[...] * ratio, acc[...] * ratio
        for score, block in zip(scores, blocks):
            weight = jnp.exp(score - now)
            part = part + jnp.sum(weight, axis=0, keepdims=True)
            update = update + dot(dot_t(pick, block).astype(BF16), weight.astype(BF16))
        total[...] = part
        acc[...] = update

    waiting = []
    for f in range(around):
        near, far = f * CORES + core, f * CORES + (CORES - 1) - core
        if f:
            arrival(near).wait_recv()
        pair_copy(f).start()
        if waiting:
            arrival(waiting[0]).wait_recv()
        absorb(waiting + [near])
        waiting = [far]
    arrival(waiting[0]).wait_recv()
    absorb(waiting)

    result = acc[...] * (1.0 / total[...])
    result = jnp.concatenate([result, result], axis=0).T
    back_out[...] = result.astype(BF16).reshape(members, t3, 128)

    def back_copy(j):
        place = chip(back_along(NEAR[j]))
        return pltpu.make_async_remote_copy(
            src_ref=back_out.at[j],
            dst_ref=back_in.at[mine],
            send_sem=back_send.at[j],
            recv_sem=back_recv.at[mine],
            device_id=device(place),
            device_id_type=MESH,
        )

    def back_arrival(j):
        place = chip(NEAR[j])
        head = head_of(place)
        return pltpu.make_async_remote_copy(
            src_ref=back_out.at[j],
            dst_ref=back_in.at[head],
            send_sem=back_send.at[j],
            recv_sem=back_recv.at[head],
            device_id=device(place),
            device_id_type=MESH,
        )

    for j in range(1, members):
        back_copy(j).start()
    back_in[mine] = back_out[0]
    for j in range(1, members):
        back_arrival(j).wait_recv()
    for pair in range(channels // (2 * HEAD)):
        even, odd = back_in[2 * pair].astype(F32), back_in[2 * pair + 1].astype(F32)
        att3[:, pair * 128 : (pair + 1) * 128] = jnp.where(low, even, odd).astype(BF16)
    loads[8].wait()
    last[...] = (x3[...].astype(F32) + dot(att3[...], w_out3[...])).astype(BF16)

    for copy in straight + edges + straight2 + edges2:
        copy.wait_send()
    for j in range(1, members):
        head_copy(j).wait_send()
        back_copy(j).wait_send()
    for f in range(around):
        if f:
            far_sent(f).wait_send()
        pair_copy(f).wait_send()


def shards(
    rows,
    cols,
    image,
    gain_fine,
    qkv_fine,
    out_fine,
    merge_fine,
    gain_mid,
    qkv_mid,
    out_mid,
    merge_mid,
    gain_coarse,
    qkv_coarse,
    out_coarse,
):
    h1, c1, w1 = image.shape
    w2, w3 = gain_mid.shape[0], gain_coarse.shape[0]
    h2, c2 = h1 // 2, c1 // 2
    h3, c3 = h2 // 2, c2 // 2
    t1, t2, t3 = h1 * c1, h2 * c2, h3 * c3
    members, around = len(NEAR), len(FAR)
    sizes = (h1, c1, h2, c2, t3, rows, cols)
    anywhere = pl.BlockSpec(memory_space=pl.ANY)

    def vmem(*shape):
        return pltpu.VMEM(shape, BF16)

    def level(tokens, width, keys, bias):
        return [
            vmem(keys, width),
            vmem(STRIP, width),
            vmem(width, width),
            vmem(tokens, width),
            vmem(keys, width),
            vmem(width, keys),
            vmem(tokens, width),
            pltpu.VMEM(bias, F32),
        ]

    def dma(*shape):
        return pltpu.SemaphoreType.DMA(shape)

    count = members * t3
    scratch = (
        [vmem(*w.shape) for w in (qkv_fine, out_fine, merge_fine, qkv_mid, out_mid, merge_mid)]
        + [vmem(*w.shape) for w in (qkv_coarse, out_coarse)]
        + [pltpu.VMEM((1, w), F32) for w in (w1, w2, w3)]
        + level(t1, w1, (h1 + 6) * c1 + STRIP, (8 * c1, 2 * c1))
        + level(t2, w2, 4 * t2, (4 * t2, t2))
        + [
            vmem(t3, w3),
            vmem(members, 2 * t3, 128),
            vmem(members, 2 * t3, 128),
            vmem(CORES * around, members, t3, 128),
            pltpu.VMEM((1, count), F32),
            pltpu.VMEM((1, count), F32),
            pltpu.VMEM((HEAD, count), F32),
            vmem(members, t3, 128),
            vmem(members, t3, 128),
            vmem(t3, w3),
        ]
        + [dma(12), dma(8), dma(8), dma(8), dma(8)]
        + [dma(members), dma(members), dma(around), dma(around), dma(CORES * around)]
        + [dma(members), dma(members), pltpu.SemaphoreType.REGULAR]
    )
    skip_fine, skip_mid, coarse_out = pl.pallas_call(
        functools.partial(kernel, sizes),
        out_shape=(vmem(t1, w1), vmem(t2, w2), vmem(t3, w3)),
        in_specs=[pl.BlockSpec(memory_space=pltpu.HBM)] * 12,
        out_specs=(pl.BlockSpec(memory_space=pltpu.VMEM),) * 3,
        scratch_shapes=scratch,
        compiler_params=pltpu.CompilerParams(
            collective_id=0, has_side_effects=True, vmem_limit_bytes=60 * 1024 * 1024
        ),
    )(
        image.reshape(t1, w1),
        gain_fine.reshape(1, w1),
        qkv_fine,
        out_fine,
        merge_fine,
        gain_mid.reshape(1, w2),
        qkv_mid,
        out_mid,
        merge_mid,
        gain_coarse.reshape(1, w3),
        qkv_coarse,
        out_coarse,
    )
    return (
        skip_fine.reshape(h1, c1, w1),
        skip_mid.reshape(h2, c2, w2),
        coarse_out.reshape(h3, c3, w3),
    )


def solution(mesh):
    placed = (P("row", "col", None),) + (P(),) * 11
    rows, cols = mesh.shape["row"], mesh.shape["col"]
    return jax.shard_map(
        functools.partial(shards, rows, cols),
        mesh=mesh,
        in_specs=placed,
        out_specs=(P("row", "col", None),) * 3,
        check_vma=False,
    )
```

```python
import functools

import jax
import jax.numpy as jnp
from jax import lax
from jax.experimental import pallas as pl
from jax.experimental.pallas import tpu as pltpu
from jax.sharding import PartitionSpec as P

MESH = pl.DeviceIdType.MESH
HEAD = 64
REACH = 3
EPSILON = 1e-06
NEG_FILL = -1e30
GROUP = 256
STRIP = 128
CORES = 2
SIDE = 4
FAR = ((0, 0, 0), (2, 2, 0), (2, 0, 2), (0, 2, 2))
NEAR = (
    (0, 0, 0),
    (1, 1, 1),
    (3, 3, 3),
    (0, 2, 0),
    (3, 3, 0),
    (3, 1, 0),
    (1, 0, 1),
    (1, 0, 3),
    (0, 3, 3),
    (0, 3, 1),
    (1, 0, 0),
    (3, 0, 0),
    (0, 1, 0),
    (0, 3, 0),
    (0, 0, 1),
    (0, 0, 3),
)
F32 = jnp.float32
BF16 = jnp.bfloat16


def iota(shape, dim):
    return lax.broadcasted_iota(jnp.int32, shape, dim)


def rms_norm(values, gains):
    wide = values.astype(F32)
    factor = lax.rsqrt(jnp.mean(wide * wide, axis=-1, keepdims=True) + EPSILON)
    return (wide * factor * gains).astype(BF16)


def dot(left, right):
    return jnp.dot(left, right, preferred_element_type=F32)


def dot_t(left, right):
    return lax.dot_general(left, right, (((1,), (1,)), ((), ())), preferred_element_type=F32)


def strip_places(slot, height, breadth):
    side = slot < 8 * height
    second = slot >= 4 * height
    across = slot & 3
    corner = slot - 8 * height
    down = corner >= 32
    along = (corner >> 2) & 3
    last = (side & second) | (~side & ((corner & 16) != 0))
    col = across + jnp.where(last, breadth - 3, 0)
    row = jnp.where(
        side,
        (slot - jnp.where(second, 4 * height, 0)) >> 2,
        along + jnp.where(down, height - 3, 0),
    )
    valid = (across < 3) & (side | ((along < 3) & (corner < 64)))
    key_col = col + jnp.where(last, -breadth, breadth)
    key_row = row + jnp.where(side, 0, jnp.where(down, -height, height))
    return row, col, key_row, key_col, valid


def strip_pick(height, breadth):
    tokens = height * breadth
    row, col, _, _, valid = strip_places(iota((STRIP, 1), 0), height, breadth)
    token = jnp.where(valid, row * breadth + col, -1)
    return jnp.where(token == iota((STRIP, tokens), 1), 1.0, 0.0).astype(BF16)


def merge_pick(tokens, breadth):
    merged = tokens // 4
    place = iota((tokens, 1), 0)
    part = place // merged
    index = place % merged
    half = breadth // 2
    token = (2 * (index // half) + part // 2) * breadth + 2 * (index % half) + part % 2
    return jnp.where(token == iota((tokens, tokens), 1), 1.0, 0.0).astype(BF16)


def merge_blocks(block, pick, weight_ref):
    tokens, channels = block.shape
    merged = tokens // 4
    grouped = dot(pick, block).astype(BF16)
    total = None
    for p in range(4):
        term = dot(
            grouped[p * merged : (p + 1) * merged], weight_ref[p * channels : (p + 1) * channels, :]
        )
        total = term if total is None else total + term
    return total.astype(BF16)


def halo_copies(
    src, own, packed, halo, above, below, strip, sends, recvs, height, breadth, here, grid
):
    row, col = here
    rows, cols = grid
    up, down = lax.rem(row + rows - 1, rows), lax.rem(row + 1, rows)
    left, right = lax.rem(col + cols - 1, cols), lax.rem(col + 1, cols)
    wide = 3 * breadth
    tall = 4 * height
    corner = 8 * height

    def copy(k, source, target, device):
        return pltpu.make_async_remote_copy(
            src_ref=source,
            dst_ref=target,
            send_sem=sends.at[k],
            recv_sem=recvs.at[k],
            device_id=device,
            device_id_type=MESH,
        )

    tokens = height * breadth
    straight = [
        copy(
            0,
            src.at[pl.ds(own, wide)],
            halo.at[pl.ds(below, wide)],
            (up, col),
        ),
        copy(
            1,
            src.at[pl.ds(own + tokens - wide, wide)],
            halo.at[pl.ds(above, wide)],
            (down, col),
        ),
    ]
    around = []
    spans = [
        (0, tall, (row, left)),
        (tall, tall, (row, right)),
        (corner, 16, (up, left)),
        (corner + 16, 16, (up, right)),
        (corner + 32, 16, (down, left)),
        (corner + 48, 16, (down, right)),
    ]
    for k, (first, count, device) in enumerate(spans):
        around.append(
            copy(
                2 + k,
                packed.at[pl.ds(first, count)],
                halo.at[pl.ds(strip + first, count)],
                device,
            )
        )
    return straight, around


def transposed(values):
    return values.astype(F32).T.astype(BF16)


def soften(parts):
    top = jnp.max(parts[0], axis=0, keepdims=True)
    for part in parts[1:]:
        top = jnp.maximum(top, jnp.max(part, axis=0, keepdims=True))
    weights = [jnp.exp(part - top) for part in parts]
    total = jnp.sum(weights[0], axis=0, keepdims=True)
    for weight in weights[1:]:
        total = total + jnp.sum(weight, axis=0, keepdims=True)
    return [weight.astype(BF16) for weight in weights], 1.0 / total


def stack_heads(queries):
    lane_head = iota((1, GROUP), 1) // HEAD
    return jnp.concatenate(
        [queries * jnp.where(lane_head == h, 1.0, 0.0).astype(BF16) for h in range(GROUP // HEAD)],
        axis=0,
    )


def head_values(terms, inverse, count):
    blocks = []
    for pair in range(GROUP // HEAD // 2):
        rows = slice(pair * 2 * HEAD, (pair + 1) * 2 * HEAD)
        lanes = slice(pair * 2 * count, (pair + 1) * 2 * count)
        both = None
        for values, weights in terms:
            term = dot(values[rows], weights[:, lanes])
            both = term if both is None else both + term
        both = both * inverse[:, lanes]
        blocks += [both[:HEAD, :count], both[HEAD:, count:]]
    return jnp.concatenate(blocks, axis=0).T.astype(BF16)


def inside_grid(key_row, key_col, height, breadth, here, grid):
    first_row, first_col = here[0] * height, here[1] * breadth
    return (
        (first_row + key_row >= 0)
        & (first_row + key_row < grid[0] * height)
        & (first_col + key_col >= 0)
        & (first_col + key_col < grid[1] * breadth)
    )


def fine_bias(bias_ref, height, breadth, here, grid):
    keys, queries = 8 * breadth, 2 * breadth
    k = iota((keys, queries), 0)
    q = iota((keys, queries), 1)
    row_gap = k // breadth - q // breadth
    col_gap = k % breadth - q % breadth
    near = (row_gap >= 0) & (row_gap <= 2 * REACH) & (jnp.abs(col_gap) <= REACH)
    key_place = k // breadth - REACH + here[0] * height
    _, _, strip_row, strip_col, valid = strip_places(iota((STRIP, 1), 0), height, breadth)
    inside = valid & inside_grid(strip_row, strip_col, height, breadth, here, grid)
    query = iota((1, queries), 1)
    strip_near = inside & (jnp.abs(strip_col - query % breadth) <= REACH)
    strip_gap = strip_row - query // breadth
    for i in range(height // 2):
        first = i * (keys + STRIP)
        place = key_place + 2 * i
        seen = near & (place >= 0) & (place < grid[0] * height)
        bias_ref[pl.ds(first, keys)] = jnp.where(seen, 0.0, NEG_FILL)
        gap = strip_gap - 2 * i
        seen = strip_near & (gap >= -REACH) & (gap <= REACH)
        bias_ref[pl.ds(first + keys, STRIP)] = jnp.where(seen, 0.0, NEG_FILL)


def fine_attention(q_ref, k_ref, vt_ref, bias_ref, att_ref, height, breadth):
    heads = GROUP // HEAD
    queries, keys = 2 * breadth, 8 * breadth
    edge = (height + 6) * breadth

    def step(i, carry):
        first = pl.multiple_of(i * queries, queries)
        bias = bias_ref[pl.ds(pl.multiple_of(i * (keys + STRIP), STRIP), keys + STRIP)]
        stacked = stack_heads(q_ref[pl.ds(first, queries), :])
        center = dot_t(k_ref[pl.ds(first, keys), :], stacked)
        center = center + jnp.concatenate([bias[:keys]] * heads, axis=1)
        strip = dot_t(k_ref[pl.ds(edge, STRIP), :], stacked)
        strip = strip + jnp.concatenate([bias[keys:]] * heads, axis=1)
        (center, strip), inverse = soften([center, strip])
        terms = [
            (vt_ref[:, pl.ds(first, keys)], center),
            (vt_ref[:, edge : edge + STRIP], strip),
        ]
        att_ref[pl.ds(first, queries), :] = head_values(terms, inverse, queries)
        return carry

    lax.fori_loop(0, height // 2, step, 0)


def mid_bias(height, breadth, here, grid):
    block = height * breadth
    wide = 3 * breadth
    k = iota((4 * block, 1), 0)
    part = k // block
    index = k % block
    row, col = index // breadth, index % breadth
    _, _, strip_row, strip_col, strip_valid = strip_places(index, height, breadth)
    is_strip = part == 3
    shift = jnp.where(part == 1, -REACH, jnp.where(part == 2, height, 0))
    key_row = jnp.where(is_strip, strip_row, row + shift)
    key_col = jnp.where(is_strip, strip_col, col)
    valid = (is_strip & strip_valid) | ((part == 0) | (~is_strip & (index < wide)))
    valid = valid & inside_grid(key_row, key_col, height, breadth, here, grid)
    q = iota((1, block), 1)
    near = (jnp.abs(key_row - q // breadth) <= REACH) & (jnp.abs(key_col - q % breadth) <= REACH)
    return jnp.where(valid & near, 0.0, NEG_FILL)


def mid_attention(q_ref, k_ref, vt_ref, bias_ref, att_ref):
    count, channels = q_ref.shape
    heads = GROUP // HEAD
    for g in range(channels // GROUP):
        lanes = slice(g * GROUP, (g + 1) * GROUP)
        score = dot_t(k_ref[:, lanes], stack_heads(q_ref[:, lanes]))
        score = score + jnp.concatenate([bias_ref[...]] * heads, axis=1)
        (weight,), inverse = soften([score])
        att_ref[:, lanes] = head_values([(vt_ref[lanes, :], weight)], inverse, count)


def kernel(
    sizes,
    image,
    gain1,
    qkv1,
    out1,
    merge1,
    gain2,
    qkv2,
    out2,
    merge2,
    gain3,
    qkv3,
    out3,
    skip1,
    skip2,
    last,
    w_qkv1,
    w_out1,
    w_merge1,
    w_qkv2,
    w_out2,
    w_merge2,
    w_qkv3,
    w_out3,
    g1,
    g2,
    g3,
    x1,
    pack1,
    turned1,
    q1,
    k1,
    vt1,
    att1,
    bias1,
    x2,
    pack2,
    turned2,
    q2,
    k2,
    vt2,
    att2,
    bias2,
    merge_pick1,
    merge_pick2,
    strip_pick2,
    x3,
    head_out,
    head_in,
    kv_all,
    top,
    total,
    acc,
    back_out,
    back_in,
    att3,
    load_sem,
    halo1_send,
    halo1_recv,
    halo2_send,
    halo2_recv,
    head_send,
    head_recv,
    far_send,
    pair_send,
    kv_recv,
    back_send,
    back_recv,
    plane_sem,
):
    h1, c1, h2, c2, t3, rows, cols = sizes
    grid = (rows, cols)
    row, col = lax.axis_index("row"), lax.axis_index("col")
    here = (row, col)
    members, around = len(NEAR), len(FAR)
    core = lax.rem(row, CORES)
    spot = (
        lax.rem(row // CORES, SIDE),
        col // 2,
        lax.rem(col, 2) * 2 + row // (CORES * SIDE),
    )

    def chip(*shifts):
        return tuple(
            lax.rem(spot[d] + sum(shift[d] for shift in shifts) % SIDE, SIDE) for d in range(3)
        )

    def device(place):
        x, y, z = place
        return (lax.rem(z, 2) * (SIDE * CORES) + x * CORES + core, y * 2 + z // 2)

    def head_of(place):
        x, y, z = place
        high = lax.rem(x // 2 + y // 2 + z // 2, 2)
        return lax.rem(x, 2) + 2 * lax.rem(y, 2) + 4 * lax.rem(z, 2) + 8 * high

    def back_along(shift):
        return tuple(-step % SIDE for step in shift)

    mine = head_of(spot)
    other = (row - core + (CORES - 1) - core, col)

    loads = [
        pltpu.make_async_copy(src, dst, load_sem.at[k])
        for k, (src, dst) in enumerate(
            [
                (image, x1.at[pl.ds(3 * c1, h1 * c1)]),
                (qkv1, w_qkv1),
                (out1, w_out1),
                (merge1, w_merge1),
                (qkv2, w_qkv2),
                (out2, w_out2),
                (merge2, w_merge2),
                (qkv3, w_qkv3),
                (out3, w_out3),
                (gain1, g1),
                (gain2, g2),
                (gain3, g3),
            ]
        )
    ]
    early = (0, 1, 9)
    for k in early:
        loads[k].start()

    barrier = pltpu.get_barrier_semaphore()

    def greet(device):
        pl.semaphore_signal(barrier, inc=1, device_id=device, device_id_type=MESH)

    for down in (rows - 1, 0, 1):
        for right in (cols - 1, 0, 1):
            if down or right:
                greet((lax.rem(row + down, rows), lax.rem(col + right, cols)))
    around_here = sorted({shift for near in NEAR[1:] for shift in (near, back_along(near))})
    for shift in around_here + list(FAR[1:]):
        greet(device(chip(shift)))
    greet(other)

    n1, n2 = h1 * c1, h2 * c2
    w1, w2 = x1.shape[1], x2.shape[1]
    own1, below1, edge1 = 3 * c1, (h1 + 3) * c1, (h1 + 6) * c1
    straight, edges = halo_copies(
        image, 0, pack1, x1, 0, below1, edge1, halo1_send, halo1_recv, h1, c1, here, grid
    )
    loads[0].wait()
    block = x1[pl.ds(own1, n1)]
    pack1[...] = dot(strip_pick(h1, c1), block).astype(BF16)
    pl.semaphore_wait(barrier, 8 + len(around_here) + around - 1 + 1)
    for copy in edges + straight:
        copy.start()
    for far in FAR[1:]:
        pl.semaphore_signal(plane_sem, inc=1, device_id=device(chip(far)), device_id_type=MESH)
    for k, load in enumerate(loads):
        if k not in early:
            load.start()
    loads[9].wait()
    loads[1].wait()
    turned1[...] = transposed(w_qkv1[:, 2 * w1 :])
    normed = rms_norm(block, g1[...])
    projected = dot(normed, w_qkv1[:, : 2 * w1])
    q1[...] = (projected[:, :w1] * HEAD ** (-0.5)).astype(BF16)
    k1[pl.ds(own1, n1)] = projected[:, w1:].astype(BF16)
    vt1[:, own1:below1] = dot_t(turned1[...], normed).astype(BF16)
    fine_bias(bias1, h1, c1, here, grid)
    merge_pick1[...] = merge_pick(n1, c1)
    merge_pick2[...] = merge_pick(n2, c2)
    strip_pick2[...] = strip_pick(h2, c2)
    for first in (n2 + 3 * c2, 2 * n2 + 3 * c2):
        x2[pl.ds(first, n2 - 3 * c2)] = jnp.zeros((n2 - 3 * c2, w2), BF16)
    used = 3 * n2 + 8 * h2 + 64
    x2[pl.ds(used, 4 * n2 - used)] = jnp.zeros((4 * n2 - used, w2), BF16)
    for copy in straight + edges:
        copy.wait_recv()
    for first, count in ((0, 3 * c1), (below1, 3 * c1), (edge1, STRIP)):
        normed = rms_norm(x1[pl.ds(first, count)], g1[...])
        k1[pl.ds(first, count)] = dot(normed, w_qkv1[:, w1 : 2 * w1]).astype(BF16)
        vt1[:, first : first + count] = dot_t(turned1[...], normed).astype(BF16)
    fine_attention(q1, k1, vt1, bias1, att1, h1, c1)
    loads[2].wait()
    skip1[...] = (x1[pl.ds(own1, n1)].astype(F32) + dot(att1[...], w_out1[...])).astype(BF16)
    loads[3].wait()
    block = merge_blocks(skip1[...], merge_pick1[...], w_merge1)

    x2[pl.ds(0, n2)] = block
    straight2, edges2 = halo_copies(
        x2, 0, pack2, x2, n2, 2 * n2, 3 * n2, halo2_send, halo2_recv, h2, c2, here, grid
    )
    pack2[...] = dot(strip_pick2[...], block).astype(BF16)
    for copy in edges2 + straight2:
        copy.start()
    loads[10].wait()
    loads[4].wait()
    turned2[...] = transposed(w_qkv2[:, 2 * w2 :])
    bias2[...] = mid_bias(h2, c2, here, grid)
    normed = rms_norm(block, g2[...])
    projected = dot(normed, w_qkv2[:, : 2 * w2])
    q2[...] = (projected[:, :w2] * HEAD ** (-0.5)).astype(BF16)
    k2[pl.ds(0, n2)] = projected[:, w2:].astype(BF16)
    vt2[:, :n2] = dot_t(turned2[...], normed).astype(BF16)
    for copy in straight2 + edges2:
        copy.wait_recv()
    normed = rms_norm(x2[pl.ds(n2, 3 * n2)], g2[...])
    k2[pl.ds(n2, 3 * n2)] = dot(normed, w_qkv2[:, w2 : 2 * w2]).astype(BF16)
    vt2[:, n2:] = dot_t(turned2[...], normed).astype(BF16)
    mid_attention(q2, k2, vt2, bias2, att2)
    loads[5].wait()
    skip2[...] = (block.astype(F32) + dot(att2[...], w_out2[...])).astype(BF16)
    loads[6].wait()
    block = merge_blocks(skip2[...], merge_pick2[...], w_merge2)
    x3[...] = block

    channels = x3.shape[1]
    loads[11].wait()
    loads[7].wait()
    projected = dot(rms_norm(block, g3[...]), w_qkv3[...])
    low = iota((1, 2 * HEAD), 1) < HEAD
    for pair in range(channels // (2 * HEAD)):
        tiles = [
            projected[:, s * channels + pair * 128 : s * channels + (pair + 1) * 128]
            for s in range(3)
        ]
        turned = [pltpu.roll(tile, HEAD, 1) for tile in tiles]
        scale = HEAD ** (-0.5)
        head_out[2 * pair, 0:t3] = jnp.where(low, tiles[0] * scale, 0.0).astype(BF16)
        head_out[2 * pair, t3:] = jnp.where(low, tiles[1], turned[2]).astype(BF16)
        head_out[2 * pair + 1, 0:t3] = jnp.where(low, turned[0] * scale, 0.0).astype(BF16)
        head_out[2 * pair + 1, t3:] = jnp.where(low, turned[1], tiles[2]).astype(BF16)

    def head_copy(j):
        place = chip(NEAR[j])
        return pltpu.make_async_remote_copy(
            src_ref=head_out.at[head_of(place)],
            dst_ref=head_in.at[j],
            send_sem=head_send.at[j],
            recv_sem=head_recv.at[j],
            device_id=device(place),
            device_id_type=MESH,
        )

    count = members * t3

    def far_copy(f, j):
        place = chip(NEAR[j], FAR[f])
        return pltpu.make_async_remote_copy(
            src_ref=head_out.at[head_of(place), pl.ds(t3, t3)],
            dst_ref=kv_all.at[f * CORES + core, j],
            send_sem=far_send.at[f],
            recv_sem=kv_recv.at[f * CORES + core],
            device_id=device(place),
            device_id_type=MESH,
        )

    def pair_copy(f):
        return pltpu.make_async_remote_copy(
            src_ref=kv_all.at[f * CORES + core],
            dst_ref=kv_all.at[f * CORES + core],
            send_sem=pair_send.at[f],
            recv_sem=kv_recv.at[f * CORES + core],
            device_id=other,
            device_id_type=MESH,
        )

    def arrival(place):
        return pltpu.make_async_remote_copy(
            src_ref=kv_all.at[place],
            dst_ref=kv_all.at[place],
            send_sem=pair_send.at[0],
            recv_sem=kv_recv.at[place],
            device_id=other,
            device_id_type=MESH,
        )

    def far_sent(f):
        return pltpu.make_async_remote_copy(
            src_ref=kv_all.at[core],
            dst_ref=kv_all.at[core],
            send_sem=far_send.at[f],
            recv_sem=kv_recv.at[core],
            device_id=other,
            device_id_type=MESH,
        )

    for j in range(1, members):
        head_copy(j).start()
    pl.semaphore_wait(plane_sem, around - 1)
    for f in range(1, around):
        for j in range(members):
            far_copy(f, j).start()
    head_in[0] = head_out[mine]
    top[...] = jnp.full(top.shape, NEG_FILL, F32)
    total[...] = jnp.zeros(total.shape, F32)
    acc[...] = jnp.zeros(acc.shape, F32)
    for j in range(1, members):
        head_copy(j).wait_recv()
    kv_all[core] = head_in[:, t3:, :]

    queries = head_in[:, 0:t3, :].reshape(count, 128)
    pick = jnp.where(iota((HEAD, 128), 0) + HEAD == iota((HEAD, 128), 1), 1.0, 0.0).astype(BF16)

    def absorb(places):
        blocks = [kv_all[place].reshape(count, 128) for place in places]
        scores = [dot_t(block, queries) for block in blocks]
        before = top[...]
        now = before
        for score in scores:
            now = jnp.maximum(now, jnp.max(score, axis=0, keepdims=True))
        ratio = jnp.exp(before - now)
        top[...] = now
        part, update = total[...] * ratio, acc[...] * ratio
        for score, block in zip(scores, blocks):
            weight = jnp.exp(score - now)
            part = part + jnp.sum(weight, axis=0, keepdims=True)
            update = update + dot(dot_t(pick, block).astype(BF16), weight.astype(BF16))
        total[...] = part
        acc[...] = update

    waiting = []
    for f in range(around):
        near, far = f * CORES + core, f * CORES + (CORES - 1) - core
        if f:
            arrival(near).wait_recv()
        pair_copy(f).start()
        if waiting:
            arrival(waiting[0]).wait_recv()
        absorb(waiting + [near])
        waiting = [far]
    arrival(waiting[0]).wait_recv()
    absorb(waiting)

    result = acc[...] * (1.0 / total[...])
    result = jnp.concatenate([result, result], axis=0).T
    back_out[...] = result.astype(BF16).reshape(members, t3, 128)

    def back_copy(j):
        place = chip(back_along(NEAR[j]))
        return pltpu.make_async_remote_copy(
            src_ref=back_out.at[j],
            dst_ref=back_in.at[mine],
            send_sem=back_send.at[j],
            recv_sem=back_recv.at[mine],
            device_id=device(place),
            device_id_type=MESH,
        )

    def back_arrival(j):
        place = chip(NEAR[j])
        head = head_of(place)
        return pltpu.make_async_remote_copy(
            src_ref=back_out.at[j],
            dst_ref=back_in.at[head],
            send_sem=back_send.at[j],
            recv_sem=back_recv.at[head],
            device_id=device(place),
            device_id_type=MESH,
        )

    for j in range(1, members):
        back_copy(j).start()
    back_in[mine] = back_out[0]
    for j in range(1, members):
        back_arrival(j).wait_recv()
    for pair in range(channels // (2 * HEAD)):
        even, odd = back_in[2 * pair].astype(F32), back_in[2 * pair + 1].astype(F32)
        att3[:, pair * 128 : (pair + 1) * 128] = jnp.where(low, even, odd).astype(BF16)
    loads[8].wait()
    last[...] = (x3[...].astype(F32) + dot(att3[...], w_out3[...])).astype(BF16)

    for copy in straight + edges + straight2 + edges2:
        copy.wait_send()
    for j in range(1, members):
        head_copy(j).wait_send()
        back_copy(j).wait_send()
    for f in range(around):
        if f:
            far_sent(f).wait_send()
        pair_copy(f).wait_send()


def shards(
    rows,
    cols,
    image,
    gain_fine,
    qkv_fine,
    out_fine,
    merge_fine,
    gain_mid,
    qkv_mid,
    out_mid,
    merge_mid,
    gain_coarse,
    qkv_coarse,
    out_coarse,
):
    h1, c1, w1 = image.shape
    w2, w3 = gain_mid.shape[0], gain_coarse.shape[0]
    h2, c2 = h1 // 2, c1 // 2
    h3, c3 = h2 // 2, c2 // 2
    t1, t2, t3 = h1 * c1, h2 * c2, h3 * c3
    members, around = len(NEAR), len(FAR)
    sizes = (h1, c1, h2, c2, t3, rows, cols)
    anywhere = pl.BlockSpec(memory_space=pl.ANY)

    def vmem(*shape):
        return pltpu.VMEM(shape, BF16)

    def level(tokens, width, keys, bias):
        return [
            vmem(keys, width),
            vmem(STRIP, width),
            vmem(width, width),
            vmem(tokens, width),
            vmem(keys, width),
            vmem(width, keys),
            vmem(tokens, width),
            pltpu.VMEM(bias, F32),
        ]

    def dma(*shape):
        return pltpu.SemaphoreType.DMA(shape)

    count = members * t3
    scratch = (
        [vmem(*w.shape) for w in (qkv_fine, out_fine, merge_fine, qkv_mid, out_mid, merge_mid)]
        + [vmem(*w.shape) for w in (qkv_coarse, out_coarse)]
        + [pltpu.VMEM((1, w), F32) for w in (w1, w2, w3)]
        + level(t1, w1, (h1 + 6) * c1 + STRIP, (h1 // 2 * (8 * c1 + STRIP), 2 * c1))
        + level(t2, w2, 4 * t2, (4 * t2, t2))
        + [vmem(t1, t1), vmem(t2, t2), vmem(STRIP, t2)]
        + [
            vmem(t3, w3),
            vmem(members, 2 * t3, 128),
            vmem(members, 2 * t3, 128),
            vmem(CORES * around, members, t3, 128),
            pltpu.VMEM((1, count), F32),
            pltpu.VMEM((1, count), F32),
            pltpu.VMEM((HEAD, count), F32),
            vmem(members, t3, 128),
            vmem(members, t3, 128),
            vmem(t3, w3),
        ]
        + [dma(12), dma(8), dma(8), dma(8), dma(8)]
        + [dma(members), dma(members), dma(around), dma(around), dma(CORES * around)]
        + [dma(members), dma(members), pltpu.SemaphoreType.REGULAR]
    )
    skip_fine, skip_mid, coarse_out = pl.pallas_call(
        functools.partial(kernel, sizes),
        out_shape=(vmem(t1, w1), vmem(t2, w2), vmem(t3, w3)),
        in_specs=[pl.BlockSpec(memory_space=pltpu.HBM)] * 12,
        out_specs=(pl.BlockSpec(memory_space=pltpu.VMEM),) * 3,
        scratch_shapes=scratch,
        compiler_params=pltpu.CompilerParams(
            collective_id=0, has_side_effects=True, vmem_limit_bytes=60 * 1024 * 1024
        ),
    )(
        image.reshape(t1, w1),
        gain_fine.reshape(1, w1),
        qkv_fine,
        out_fine,
        merge_fine,
        gain_mid.reshape(1, w2),
        qkv_mid,
        out_mid,
        merge_mid,
        gain_coarse.reshape(1, w3),
        qkv_coarse,
        out_coarse,
    )
    return (
        skip_fine.reshape(h1, c1, w1),
        skip_mid.reshape(h2, c2, w2),
        coarse_out.reshape(h3, c3, w3),
    )


def solution(mesh):
    placed = (P("row", "col", None),) + (P(),) * 11
    rows, cols = mesh.shape["row"], mesh.shape["col"]
    return jax.shard_map(
        functools.partial(shards, rows, cols),
        mesh=mesh,
        in_specs=placed,
        out_specs=(P("row", "col", None),) * 3,
        check_vma=False,
    )
```

```python
import functools

import jax
import jax.numpy as jnp
from jax import lax
from jax.experimental import pallas as pl
from jax.experimental.pallas import tpu as pltpu
from jax.sharding import PartitionSpec as P

MESH = pl.DeviceIdType.MESH
HEAD = 64
REACH = 3
EPSILON = 1e-06
NEG_FILL = -1e30
GROUP = 256
STRIP = 128
CORES = 2
SIDE = 4
FAR = ((0, 0, 0), (2, 2, 0), (2, 0, 2), (0, 2, 2))
NEAR = (
    (0, 0, 0),
    (1, 1, 1),
    (3, 3, 3),
    (0, 2, 0),
    (3, 3, 0),
    (3, 1, 0),
    (1, 0, 1),
    (1, 0, 3),
    (0, 3, 3),
    (0, 3, 1),
    (1, 0, 0),
    (3, 0, 0),
    (0, 1, 0),
    (0, 3, 0),
    (0, 0, 1),
    (0, 0, 3),
)
F32 = jnp.float32
BF16 = jnp.bfloat16


def iota(shape, dim):
    return lax.broadcasted_iota(jnp.int32, shape, dim)


def rms_norm(values, gains):
    wide = values.astype(F32)
    factor = lax.rsqrt(jnp.mean(wide * wide, axis=-1, keepdims=True) + EPSILON)
    return (wide * factor * gains).astype(BF16)


def dot(left, right):
    return jnp.dot(left, right, preferred_element_type=F32)


def dot_t(left, right):
    return lax.dot_general(left, right, (((1,), (1,)), ((), ())), preferred_element_type=F32)


def strip_places(slot, height, breadth):
    side = slot < 8 * height
    second = slot >= 4 * height
    across = slot & 3
    corner = slot - 8 * height
    down = corner >= 32
    along = (corner >> 2) & 3
    last = (side & second) | (~side & ((corner & 16) != 0))
    col = across + jnp.where(last, breadth - 3, 0)
    row = jnp.where(
        side,
        (slot - jnp.where(second, 4 * height, 0)) >> 2,
        along + jnp.where(down, height - 3, 0),
    )
    valid = (across < 3) & (side | ((along < 3) & (corner < 64)))
    key_col = col + jnp.where(last, -breadth, breadth)
    key_row = row + jnp.where(side, 0, jnp.where(down, -height, height))
    return row, col, key_row, key_col, valid


def strip_pick(height, breadth):
    tokens = height * breadth
    row, col, _, _, valid = strip_places(iota((STRIP, 1), 0), height, breadth)
    token = jnp.where(valid, row * breadth + col, -1)
    return jnp.where(token == iota((STRIP, tokens), 1), 1.0, 0.0).astype(BF16)


def merge_pick(tokens, breadth):
    merged = tokens // 4
    place = iota((tokens, 1), 0)
    part = place // merged
    index = place % merged
    half = breadth // 2
    token = (2 * (index // half) + part // 2) * breadth + 2 * (index % half) + part % 2
    return jnp.where(token == iota((tokens, tokens), 1), 1.0, 0.0).astype(BF16)


def merge_blocks(block, pick, weight_ref):
    tokens, channels = block.shape
    merged = tokens // 4
    grouped = dot(pick, block).astype(BF16)
    total = None
    for p in range(4):
        term = dot(
            grouped[p * merged : (p + 1) * merged], weight_ref[p * channels : (p + 1) * channels, :]
        )
        total = term if total is None else total + term
    return total.astype(BF16)


def halo_copies(
    src, own, packed, halo, above, below, strip, sends, recvs, height, breadth, here, grid
):
    row, col = here
    rows, cols = grid
    up, down = lax.rem(row + rows - 1, rows), lax.rem(row + 1, rows)
    left, right = lax.rem(col + cols - 1, cols), lax.rem(col + 1, cols)
    wide = 3 * breadth
    tall = 4 * height
    corner = 8 * height

    def copy(k, source, target, device):
        return pltpu.make_async_remote_copy(
            src_ref=source,
            dst_ref=target,
            send_sem=sends.at[k],
            recv_sem=recvs.at[k],
            device_id=device,
            device_id_type=MESH,
        )

    tokens = height * breadth
    straight = [
        copy(
            0,
            src.at[pl.ds(own, wide)],
            halo.at[pl.ds(below, wide)],
            (up, col),
        ),
        copy(
            1,
            src.at[pl.ds(own + tokens - wide, wide)],
            halo.at[pl.ds(above, wide)],
            (down, col),
        ),
    ]
    around = []
    spans = [
        (0, tall, (row, left)),
        (tall, tall, (row, right)),
        (corner, 16, (up, left)),
        (corner + 16, 16, (up, right)),
        (corner + 32, 16, (down, left)),
        (corner + 48, 16, (down, right)),
    ]
    for k, (first, count, device) in enumerate(spans):
        around.append(
            copy(
                2 + k,
                packed.at[pl.ds(first, count)],
                halo.at[pl.ds(strip + first, count)],
                device,
            )
        )
    return straight, around


def transposed(values):
    return values.astype(F32).T.astype(BF16)


def soften(parts):
    top = jnp.max(parts[0], axis=0, keepdims=True)
    for part in parts[1:]:
        top = jnp.maximum(top, jnp.max(part, axis=0, keepdims=True))
    weights = [jnp.exp(part - top) for part in parts]
    total = jnp.sum(weights[0], axis=0, keepdims=True)
    for weight in weights[1:]:
        total = total + jnp.sum(weight, axis=0, keepdims=True)
    return [weight.astype(BF16) for weight in weights], 1.0 / total


def stack_heads(queries):
    lane_head = iota((1, GROUP), 1) // HEAD
    return jnp.concatenate(
        [queries * jnp.where(lane_head == h, 1.0, 0.0).astype(BF16) for h in range(GROUP // HEAD)],
        axis=0,
    )


def head_sums(terms, count):
    blocks = []
    for pair in range(GROUP // HEAD // 2):
        rows = slice(pair * 2 * HEAD, (pair + 1) * 2 * HEAD)
        lanes = slice(pair * 2 * count, (pair + 1) * 2 * count)
        both = None
        for values, weights in terms:
            term = dot(values[rows], weights[:, lanes])
            both = term if both is None else both + term
        blocks += [both[:HEAD, :count], both[HEAD:, count:]]
    return blocks


def scaled(blocks, factor, count):
    return [block * factor[:, h * count : (h + 1) * count] for h, block in enumerate(blocks)]


def inside_grid(key_row, key_col, height, breadth, here, grid):
    first_row, first_col = here[0] * height, here[1] * breadth
    return (
        (first_row + key_row >= 0)
        & (first_row + key_row < grid[0] * height)
        & (first_col + key_col >= 0)
        & (first_col + key_col < grid[1] * breadth)
    )


def fine_bias(bias_ref, height, breadth, here, grid):
    own, rows, queries = height * breadth, 4 * breadth, 2 * breadth
    k = iota((own, queries), 0)
    q = iota((own, queries), 1)
    row_gap = k // breadth - q // breadth
    near = jnp.abs(k % breadth - q % breadth) <= REACH
    index = iota((rows, 1), 0)
    query = iota((1, queries), 1)
    halo_near = jnp.abs(index % breadth - query % breadth) <= REACH
    _, _, strip_row, strip_col, valid = strip_places(iota((STRIP, 1), 0), height, breadth)
    inside = valid & inside_grid(strip_row, strip_col, height, breadth, here, grid)
    strip_near = inside & (jnp.abs(strip_col - query % breadth) <= REACH)
    for i in range(height // 2):
        first = i * (own + rows + STRIP)
        gap = row_gap - 2 * i
        seen = near & (gap >= -REACH) & (gap <= REACH)
        bias_ref[pl.ds(first, own)] = jnp.where(seen, 0.0, NEG_FILL)
        key_row = index // breadth + (-REACH if i < height // 4 else height)
        inside = (index < 3 * breadth) & inside_grid(
            key_row, index % breadth, height, breadth, here, grid
        )
        gap = key_row - query // breadth - 2 * i
        seen = halo_near & inside & (gap >= -REACH) & (gap <= REACH)
        bias_ref[pl.ds(first + own, rows)] = jnp.where(seen, 0.0, NEG_FILL)
        gap = strip_row - query // breadth - 2 * i
        seen = strip_near & (gap >= -REACH) & (gap <= REACH)
        bias_ref[pl.ds(first + own + rows, STRIP)] = jnp.where(seen, 0.0, NEG_FILL)


def fine_own(q_ref, k_ref, vt_ref, bias_ref, top_ref, total_ref, sum_ref, height, breadth):
    heads = GROUP // HEAD
    queries, own, rows = 2 * breadth, height * breadth, 4 * breadth

    def step(i, carry):
        first = pl.multiple_of(i * queries, queries)
        start = pl.multiple_of(i * (own + rows + STRIP), STRIP)
        score = dot_t(k_ref[:own, :], stack_heads(q_ref[pl.ds(first, queries), :]))
        score = score + jnp.concatenate([bias_ref[pl.ds(start, own)]] * heads, axis=1)
        top = jnp.max(score, axis=0, keepdims=True)
        weight = jnp.exp(score - top)
        top_ref[i] = top
        total_ref[i] = jnp.sum(weight, axis=0, keepdims=True)
        sums = head_sums([(vt_ref[:, :own], weight.astype(BF16))], queries)
        sum_ref[i] = jnp.concatenate(sums, axis=0)
        return carry

    lax.fori_loop(0, height // 2, step, 0)


def fine_rest(q_ref, k_ref, vt_ref, bias_ref, top_ref, total_ref, sum_ref, att_ref, height, breadth):
    heads = GROUP // HEAD
    queries, own, rows = 2 * breadth, height * breadth, 4 * breadth
    edge = own + 2 * rows

    def step(i, carry):
        first = pl.multiple_of(i * queries, queries)
        start = pl.multiple_of(i * (own + rows + STRIP), STRIP)
        side = pl.multiple_of(own + rows * (i // (height // 4)), STRIP)
        stacked = stack_heads(q_ref[pl.ds(first, queries), :])
        halo = dot_t(k_ref[pl.ds(side, rows), :], stacked)
        halo = halo + jnp.concatenate([bias_ref[pl.ds(start + own, rows)]] * heads, axis=1)
        strip = dot_t(k_ref[pl.ds(edge, STRIP), :], stacked)
        strip = strip + jnp.concatenate([bias_ref[pl.ds(start + own + rows, STRIP)]] * heads, axis=1)
        before = top_ref[i]
        top = jnp.maximum(before, jnp.max(halo, axis=0, keepdims=True))
        top = jnp.maximum(top, jnp.max(strip, axis=0, keepdims=True))
        ratio = jnp.exp(before - top)
        halo = jnp.exp(halo - top)
        strip = jnp.exp(strip - top)
        total = total_ref[i] * ratio + jnp.sum(halo, axis=0, keepdims=True)
        total = total + jnp.sum(strip, axis=0, keepdims=True)
        terms = [
            (vt_ref[:, pl.ds(side, rows)], halo.astype(BF16)),
            (vt_ref[:, edge : edge + STRIP], strip.astype(BF16)),
        ]
        known = sum_ref[i]
        known = [known[h * HEAD : (h + 1) * HEAD] for h in range(heads)]
        sums = [a + b for a, b in zip(scaled(known, ratio, queries), head_sums(terms, queries))]
        sums = jnp.concatenate(scaled(sums, 1.0 / total, queries), axis=0)
        att_ref[pl.ds(first, queries), :] = sums.T.astype(BF16)
        return carry

    lax.fori_loop(0, height // 2, step, 0)


def mid_bias(height, breadth, here, grid):
    block = height * breadth
    wide = 3 * breadth
    k = iota((4 * block, 1), 0)
    part = k // block
    index = k % block
    row, col = index // breadth, index % breadth
    _, _, strip_row, strip_col, strip_valid = strip_places(index, height, breadth)
    is_strip = part == 3
    shift = jnp.where(part == 1, -REACH, jnp.where(part == 2, height, 0))
    key_row = jnp.where(is_strip, strip_row, row + shift)
    key_col = jnp.where(is_strip, strip_col, col)
    valid = (is_strip & strip_valid) | ((part == 0) | (~is_strip & (index < wide)))
    valid = valid & inside_grid(key_row, key_col, height, breadth, here, grid)
    q = iota((1, block), 1)
    near = (jnp.abs(key_row - q // breadth) <= REACH) & (jnp.abs(key_col - q % breadth) <= REACH)
    return jnp.where(valid & near, 0.0, NEG_FILL)


def mid_attention(q_ref, k_ref, vt_ref, bias_ref, att_ref):
    count, channels = q_ref.shape
    heads = GROUP // HEAD
    for g in range(channels // GROUP):
        lanes = slice(g * GROUP, (g + 1) * GROUP)
        score = dot_t(k_ref[:, lanes], stack_heads(q_ref[:, lanes]))
        score = score + jnp.concatenate([bias_ref[...]] * heads, axis=1)
        (weight,), inverse = soften([score])
        sums = scaled(head_sums([(vt_ref[lanes, :], weight)], count), inverse, count)
        att_ref[:, lanes] = jnp.concatenate(sums, axis=0).T.astype(BF16)


def kernel(
    sizes,
    image,
    gain1,
    qkv1,
    out1,
    merge1,
    gain2,
    qkv2,
    out2,
    merge2,
    gain3,
    qkv3,
    out3,
    skip1,
    skip2,
    last,
    w_qkv1,
    w_out1,
    w_merge1,
    w_qkv2,
    w_out2,
    w_merge2,
    w_qkv3,
    w_out3,
    g1,
    g2,
    g3,
    x1,
    pack1,
    turned1,
    q1,
    k1,
    vt1,
    att1,
    bias1,
    top1,
    total1,
    sum1,
    x2,
    pack2,
    turned2,
    q2,
    k2,
    vt2,
    att2,
    bias2,
    merge_pick1,
    merge_pick2,
    strip_pick2,
    x3,
    head_out,
    head_in,
    kv_all,
    top,
    total,
    acc,
    back_out,
    back_in,
    att3,
    load_sem,
    halo1_send,
    halo1_recv,
    halo2_send,
    halo2_recv,
    head_send,
    head_recv,
    far_send,
    pair_send,
    kv_recv,
    back_send,
    back_recv,
    plane_sem,
):
    h1, c1, h2, c2, t3, rows, cols = sizes
    grid = (rows, cols)
    row, col = lax.axis_index("row"), lax.axis_index("col")
    here = (row, col)
    members, around = len(NEAR), len(FAR)
    core = lax.rem(row, CORES)
    spot = (
        lax.rem(row // CORES, SIDE),
        col // 2,
        lax.rem(col, 2) * 2 + row // (CORES * SIDE),
    )

    def chip(*shifts):
        return tuple(
            lax.rem(spot[d] + sum(shift[d] for shift in shifts) % SIDE, SIDE) for d in range(3)
        )

    def device(place):
        x, y, z = place
        return (lax.rem(z, 2) * (SIDE * CORES) + x * CORES + core, y * 2 + z // 2)

    def head_of(place):
        x, y, z = place
        high = lax.rem(x // 2 + y // 2 + z // 2, 2)
        return lax.rem(x, 2) + 2 * lax.rem(y, 2) + 4 * lax.rem(z, 2) + 8 * high

    def back_along(shift):
        return tuple(-step % SIDE for step in shift)

    mine = head_of(spot)
    other = (row - core + (CORES - 1) - core, col)

    loads = [
        pltpu.make_async_copy(src, dst, load_sem.at[k])
        for k, (src, dst) in enumerate(
            [
                (image, x1.at[pl.ds(0, h1 * c1)]),
                (qkv1, w_qkv1),
                (out1, w_out1),
                (merge1, w_merge1),
                (qkv2, w_qkv2),
                (out2, w_out2),
                (merge2, w_merge2),
                (qkv3, w_qkv3),
                (out3, w_out3),
                (gain1, g1),
                (gain2, g2),
                (gain3, g3),
            ]
        )
    ]
    early = (0, 1, 9)
    for k in early:
        loads[k].start()

    barrier = pltpu.get_barrier_semaphore()

    def greet(device):
        pl.semaphore_signal(barrier, inc=1, device_id=device, device_id_type=MESH)

    for down in (rows - 1, 0, 1):
        for right in (cols - 1, 0, 1):
            if down or right:
                greet((lax.rem(row + down, rows), lax.rem(col + right, cols)))
    around_here = sorted({shift for near in NEAR[1:] for shift in (near, back_along(near))})
    for shift in around_here + list(FAR[1:]):
        greet(device(chip(shift)))
    greet(other)

    n1, n2 = h1 * c1, h2 * c2
    w1, w2 = x1.shape[1], x2.shape[1]
    above1, below1, edge1 = n1, n1 + 4 * c1, n1 + 8 * c1
    for first in (above1 + 3 * c1, below1 + 3 * c1):
        x1[pl.ds(first, c1)] = jnp.zeros((c1, w1), BF16)
    straight, edges = halo_copies(
        image, 0, pack1, x1, above1, below1, edge1, halo1_send, halo1_recv, h1, c1, here, grid
    )
    loads[0].wait()
    block = x1[pl.ds(0, n1)]
    pack1[...] = dot(strip_pick(h1, c1), block).astype(BF16)
    pl.semaphore_wait(barrier, 8 + len(around_here) + around - 1 + 1)
    for copy in edges + straight:
        copy.start()
    for far in FAR[1:]:
        pl.semaphore_signal(plane_sem, inc=1, device_id=device(chip(far)), device_id_type=MESH)
    for k, load in enumerate(loads):
        if k not in early:
            load.start()
    loads[9].wait()
    loads[1].wait()
    turned1[...] = transposed(w_qkv1[:, 2 * w1 :])
    normed = rms_norm(block, g1[...])
    projected = dot(normed, w_qkv1[:, : 2 * w1])
    q1[...] = (projected[:, :w1] * HEAD ** (-0.5)).astype(BF16)
    k1[pl.ds(0, n1)] = projected[:, w1:].astype(BF16)
    vt1[:, :n1] = dot_t(turned1[...], normed).astype(BF16)
    fine_bias(bias1, h1, c1, here, grid)
    merge_pick1[...] = merge_pick(n1, c1)
    merge_pick2[...] = merge_pick(n2, c2)
    strip_pick2[...] = strip_pick(h2, c2)
    for first in (n2 + 3 * c2, 2 * n2 + 3 * c2):
        x2[pl.ds(first, n2 - 3 * c2)] = jnp.zeros((n2 - 3 * c2, w2), BF16)
    used = 3 * n2 + 8 * h2 + 64
    x2[pl.ds(used, 4 * n2 - used)] = jnp.zeros((4 * n2 - used, w2), BF16)
    fine_own(q1, k1, vt1, bias1, top1, total1, sum1, h1, c1)
    for copy in straight + edges:
        copy.wait_recv()
    normed = rms_norm(x1[pl.ds(n1, 8 * c1 + STRIP)], g1[...])
    k1[pl.ds(n1, 8 * c1 + STRIP)] = dot(normed, w_qkv1[:, w1 : 2 * w1]).astype(BF16)
    vt1[:, n1:] = dot_t(turned1[...], normed).astype(BF16)
    fine_rest(q1, k1, vt1, bias1, top1, total1, sum1, att1, h1, c1)
    loads[2].wait()
    skip1[...] = (x1[pl.ds(0, n1)].astype(F32) + dot(att1[...], w_out1[...])).astype(BF16)
    loads[3].wait()
    block = merge_blocks(skip1[...], merge_pick1[...], w_merge1)

    x2[pl.ds(0, n2)] = block
    straight2, edges2 = halo_copies(
        x2, 0, pack2, x2, n2, 2 * n2, 3 * n2, halo2_send, halo2_recv, h2, c2, here, grid
    )
    pack2[...] = dot(strip_pick2[...], block).astype(BF16)
    for copy in edges2 + straight2:
        copy.start()
    loads[10].wait()
    loads[4].wait()
    turned2[...] = transposed(w_qkv2[:, 2 * w2 :])
    bias2[...] = mid_bias(h2, c2, here, grid)
    normed = rms_norm(block, g2[...])
    projected = dot(normed, w_qkv2[:, : 2 * w2])
    q2[...] = (projected[:, :w2] * HEAD ** (-0.5)).astype(BF16)
    k2[pl.ds(0, n2)] = projected[:, w2:].astype(BF16)
    vt2[:, :n2] = dot_t(turned2[...], normed).astype(BF16)
    for copy in straight2 + edges2:
        copy.wait_recv()
    normed = rms_norm(x2[pl.ds(n2, 3 * n2)], g2[...])
    k2[pl.ds(n2, 3 * n2)] = dot(normed, w_qkv2[:, w2 : 2 * w2]).astype(BF16)
    vt2[:, n2:] = dot_t(turned2[...], normed).astype(BF16)
    mid_attention(q2, k2, vt2, bias2, att2)
    loads[5].wait()
    skip2[...] = (block.astype(F32) + dot(att2[...], w_out2[...])).astype(BF16)
    loads[6].wait()
    block = merge_blocks(skip2[...], merge_pick2[...], w_merge2)
    x3[...] = block

    channels = x3.shape[1]
    loads[11].wait()
    loads[7].wait()
    projected = dot(rms_norm(block, g3[...]), w_qkv3[...])
    low = iota((1, 2 * HEAD), 1) < HEAD
    for pair in range(channels // (2 * HEAD)):
        tiles = [
            projected[:, s * channels + pair * 128 : s * channels + (pair + 1) * 128]
            for s in range(3)
        ]
        turned = [pltpu.roll(tile, HEAD, 1) for tile in tiles]
        scale = HEAD ** (-0.5)
        head_out[2 * pair, 0:t3] = jnp.where(low, tiles[0] * scale, 0.0).astype(BF16)
        head_out[2 * pair, t3:] = jnp.where(low, tiles[1], turned[2]).astype(BF16)
        head_out[2 * pair + 1, 0:t3] = jnp.where(low, turned[0] * scale, 0.0).astype(BF16)
        head_out[2 * pair + 1, t3:] = jnp.where(low, turned[1], tiles[2]).astype(BF16)

    def head_copy(j):
        place = chip(NEAR[j])
        return pltpu.make_async_remote_copy(
            src_ref=head_out.at[head_of(place)],
            dst_ref=head_in.at[j],
            send_sem=head_send.at[j],
            recv_sem=head_recv.at[j],
            device_id=device(place),
            device_id_type=MESH,
        )

    count = members * t3

    def far_copy(f, j):
        place = chip(NEAR[j], FAR[f])
        return pltpu.make_async_remote_copy(
            src_ref=head_out.at[head_of(place), pl.ds(t3, t3)],
            dst_ref=kv_all.at[f * CORES + core, j],
            send_sem=far_send.at[f],
            recv_sem=kv_recv.at[f * CORES + core],
            device_id=device(place),
            device_id_type=MESH,
        )

    def pair_copy(f):
        return pltpu.make_async_remote_copy(
            src_ref=kv_all.at[f * CORES + core],
            dst_ref=kv_all.at[f * CORES + core],
            send_sem=pair_send.at[f],
            recv_sem=kv_recv.at[f * CORES + core],
            device_id=other,
            device_id_type=MESH,
        )

    def arrival(place):
        return pltpu.make_async_remote_copy(
            src_ref=kv_all.at[place],
            dst_ref=kv_all.at[place],
            send_sem=pair_send.at[0],
            recv_sem=kv_recv.at[place],
            device_id=other,
            device_id_type=MESH,
        )

    def far_sent(f):
        return pltpu.make_async_remote_copy(
            src_ref=kv_all.at[core],
            dst_ref=kv_all.at[core],
            send_sem=far_send.at[f],
            recv_sem=kv_recv.at[core],
            device_id=other,
            device_id_type=MESH,
        )

    for j in range(1, members):
        head_copy(j).start()
    pl.semaphore_wait(plane_sem, around - 1)
    for f in range(1, around):
        for j in range(members):
            far_copy(f, j).start()
    head_in[0] = head_out[mine]
    top[...] = jnp.full(top.shape, NEG_FILL, F32)
    total[...] = jnp.zeros(total.shape, F32)
    acc[...] = jnp.zeros(acc.shape, F32)
    for j in range(1, members):
        head_copy(j).wait_recv()
    kv_all[core] = head_in[:, t3:, :]

    queries = head_in[:, 0:t3, :].reshape(count, 128)
    pick = jnp.where(iota((HEAD, 128), 0) + HEAD == iota((HEAD, 128), 1), 1.0, 0.0).astype(BF16)

    def absorb(places):
        blocks = [kv_all[place].reshape(count, 128) for place in places]
        scores = [dot_t(block, queries) for block in blocks]
        before = top[...]
        now = before
        for score in scores:
            now = jnp.maximum(now, jnp.max(score, axis=0, keepdims=True))
        ratio = jnp.exp(before - now)
        top[...] = now
        part, update = total[...] * ratio, acc[...] * ratio
        for score, block in zip(scores, blocks):
            weight = jnp.exp(score - now)
            part = part + jnp.sum(weight, axis=0, keepdims=True)
            update = update + dot(dot_t(pick, block).astype(BF16), weight.astype(BF16))
        total[...] = part
        acc[...] = update

    waiting = []
    for f in range(around):
        near, far = f * CORES + core, f * CORES + (CORES - 1) - core
        if f:
            arrival(near).wait_recv()
        pair_copy(f).start()
        if waiting:
            arrival(waiting[0]).wait_recv()
        absorb(waiting + [near])
        waiting = [far]
    arrival(waiting[0]).wait_recv()
    absorb(waiting)

    result = acc[...] * (1.0 / total[...])
    result = jnp.concatenate([result, result], axis=0).T
    back_out[...] = result.astype(BF16).reshape(members, t3, 128)

    def back_copy(j):
        place = chip(back_along(NEAR[j]))
        return pltpu.make_async_remote_copy(
            src_ref=back_out.at[j],
            dst_ref=back_in.at[mine],
            send_sem=back_send.at[j],
            recv_sem=back_recv.at[mine],
            device_id=device(place),
            device_id_type=MESH,
        )

    def back_arrival(j):
        place = chip(NEAR[j])
        head = head_of(place)
        return pltpu.make_async_remote_copy(
            src_ref=back_out.at[j],
            dst_ref=back_in.at[head],
            send_sem=back_send.at[j],
            recv_sem=back_recv.at[head],
            device_id=device(place),
            device_id_type=MESH,
        )

    for j in range(1, members):
        back_copy(j).start()
    back_in[mine] = back_out[0]
    for j in range(1, members):
        back_arrival(j).wait_recv()
    for pair in range(channels // (2 * HEAD)):
        even, odd = back_in[2 * pair].astype(F32), back_in[2 * pair + 1].astype(F32)
        att3[:, pair * 128 : (pair + 1) * 128] = jnp.where(low, even, odd).astype(BF16)
    loads[8].wait()
    last[...] = (x3[...].astype(F32) + dot(att3[...], w_out3[...])).astype(BF16)

    for copy in straight + edges + straight2 + edges2:
        copy.wait_send()
    for j in range(1, members):
        head_copy(j).wait_send()
        back_copy(j).wait_send()
    for f in range(around):
        if f:
            far_sent(f).wait_send()
        pair_copy(f).wait_send()


def shards(
    rows,
    cols,
    image,
    gain_fine,
    qkv_fine,
    out_fine,
    merge_fine,
    gain_mid,
    qkv_mid,
    out_mid,
    merge_mid,
    gain_coarse,
    qkv_coarse,
    out_coarse,
):
    h1, c1, w1 = image.shape
    w2, w3 = gain_mid.shape[0], gain_coarse.shape[0]
    h2, c2 = h1 // 2, c1 // 2
    h3, c3 = h2 // 2, c2 // 2
    t1, t2, t3 = h1 * c1, h2 * c2, h3 * c3
    members, around = len(NEAR), len(FAR)
    sizes = (h1, c1, h2, c2, t3, rows, cols)
    anywhere = pl.BlockSpec(memory_space=pl.ANY)

    def vmem(*shape):
        return pltpu.VMEM(shape, BF16)

    def level(tokens, width, keys, bias):
        return [
            vmem(keys, width),
            vmem(STRIP, width),
            vmem(width, width),
            vmem(tokens, width),
            vmem(keys, width),
            vmem(width, keys),
            vmem(tokens, width),
            pltpu.VMEM(bias, F32),
        ]

    def dma(*shape):
        return pltpu.SemaphoreType.DMA(shape)

    count = members * t3
    scratch = (
        [vmem(*w.shape) for w in (qkv_fine, out_fine, merge_fine, qkv_mid, out_mid, merge_mid)]
        + [vmem(*w.shape) for w in (qkv_coarse, out_coarse)]
        + [pltpu.VMEM((1, w), F32) for w in (w1, w2, w3)]
        + level(t1, w1, t1 + 8 * c1 + STRIP, (h1 // 2 * (t1 + 4 * c1 + STRIP), 2 * c1))
        + [
            pltpu.VMEM((h1 // 2, 1, w1 // HEAD * 2 * c1), F32),
            pltpu.VMEM((h1 // 2, 1, w1 // HEAD * 2 * c1), F32),
            pltpu.VMEM((h1 // 2, w1, 2 * c1), F32),
        ]
        + level(t2, w2, 4 * t2, (4 * t2, t2))
        + [vmem(t1, t1), vmem(t2, t2), vmem(STRIP, t2)]
        + [
            vmem(t3, w3),
            vmem(members, 2 * t3, 128),
            vmem(members, 2 * t3, 128),
            vmem(CORES * around, members, t3, 128),
            pltpu.VMEM((1, count), F32),
            pltpu.VMEM((1, count), F32),
            pltpu.VMEM((HEAD, count), F32),
            vmem(members, t3, 128),
            vmem(members, t3, 128),
            vmem(t3, w3),
        ]
        + [dma(12), dma(8), dma(8), dma(8), dma(8)]
        + [dma(members), dma(members), dma(around), dma(around), dma(CORES * around)]
        + [dma(members), dma(members), pltpu.SemaphoreType.REGULAR]
    )
    skip_fine, skip_mid, coarse_out = pl.pallas_call(
        functools.partial(kernel, sizes),
        out_shape=(vmem(t1, w1), vmem(t2, w2), vmem(t3, w3)),
        in_specs=[pl.BlockSpec(memory_space=pltpu.HBM)] * 12,
        out_specs=(pl.BlockSpec(memory_space=pltpu.VMEM),) * 3,
        scratch_shapes=scratch,
        compiler_params=pltpu.CompilerParams(
            collective_id=0, has_side_effects=True, vmem_limit_bytes=60 * 1024 * 1024
        ),
    )(
        image.reshape(t1, w1),
        gain_fine.reshape(1, w1),
        qkv_fine,
        out_fine,
        merge_fine,
        gain_mid.reshape(1, w2),
        qkv_mid,
        out_mid,
        merge_mid,
        gain_coarse.reshape(1, w3),
        qkv_coarse,
        out_coarse,
    )
    return (
        skip_fine.reshape(h1, c1, w1),
        skip_mid.reshape(h2, c2, w2),
        coarse_out.reshape(h3, c3, w3),
    )


def solution(mesh):
    placed = (P("row", "col", None),) + (P(),) * 11
    rows, cols = mesh.shape["row"], mesh.shape["col"]
    return jax.shard_map(
        functools.partial(shards, rows, cols),
        mesh=mesh,
        in_specs=placed,
        out_specs=(P("row", "col", None),) * 3,
        check_vma=False,
    )
```

```python
import functools

import jax
import jax.numpy as jnp
from jax import lax
from jax.experimental import pallas as pl
from jax.experimental.pallas import tpu as pltpu
from jax.sharding import PartitionSpec as P

MESH = pl.DeviceIdType.MESH
HEAD = 64
REACH = 3
EPSILON = 1e-06
NEG_FILL = -1e30
GROUP = 256
STRIP = 128
CORES = 2
SIDE = 4
FAR = ((0, 0, 0), (2, 2, 0), (2, 0, 2), (0, 2, 2))
NEAR = (
    (0, 0, 0),
    (1, 1, 1),
    (3, 3, 3),
    (0, 2, 0),
    (3, 3, 0),
    (3, 1, 0),
    (1, 0, 1),
    (1, 0, 3),
    (0, 3, 3),
    (0, 3, 1),
    (1, 0, 0),
    (3, 0, 0),
    (0, 1, 0),
    (0, 3, 0),
    (0, 0, 1),
    (0, 0, 3),
)
F32 = jnp.float32
BF16 = jnp.bfloat16


def iota(shape, dim):
    return lax.broadcasted_iota(jnp.int32, shape, dim)


def rms_norm(values, gains):
    wide = values.astype(F32)
    factor = lax.rsqrt(jnp.mean(wide * wide, axis=-1, keepdims=True) + EPSILON)
    return (wide * factor * gains).astype(BF16)


def dot(left, right):
    return jnp.dot(left, right, preferred_element_type=F32)


def dot_t(left, right):
    return lax.dot_general(left, right, (((1,), (1,)), ((), ())), preferred_element_type=F32)


def strip_places(slot, height, breadth):
    side = slot < 8 * height
    second = slot >= 4 * height
    across = slot & 3
    corner = slot - 8 * height
    down = corner >= 32
    along = (corner >> 2) & 3
    last = (side & second) | (~side & ((corner & 16) != 0))
    col = across + jnp.where(last, breadth - 3, 0)
    row = jnp.where(
        side,
        (slot - jnp.where(second, 4 * height, 0)) >> 2,
        along + jnp.where(down, height - 3, 0),
    )
    valid = (across < 3) & (side | ((along < 3) & (corner < 64)))
    key_col = col + jnp.where(last, -breadth, breadth)
    key_row = row + jnp.where(side, 0, jnp.where(down, -height, height))
    return row, col, key_row, key_col, valid


def strip_pick(height, breadth):
    tokens = height * breadth
    row, col, _, _, valid = strip_places(iota((STRIP, 1), 0), height, breadth)
    token = jnp.where(valid, row * breadth + col, -1)
    return jnp.where(token == iota((STRIP, tokens), 1), 1.0, 0.0).astype(BF16)


def merge_pick(tokens, breadth):
    merged = tokens // 4
    place = iota((tokens, 1), 0)
    part = place // merged
    index = place % merged
    half = breadth // 2
    token = (2 * (index // half) + part // 2) * breadth + 2 * (index % half) + part % 2
    return jnp.where(token == iota((tokens, tokens), 1), 1.0, 0.0).astype(BF16)


def merge_blocks(block, pick, weight_ref):
    tokens, channels = block.shape
    merged = tokens // 4
    grouped = dot(pick, block).astype(BF16)
    total = None
    for p in range(4):
        term = dot(
            grouped[p * merged : (p + 1) * merged], weight_ref[p * channels : (p + 1) * channels, :]
        )
        total = term if total is None else total + term
    return total.astype(BF16)


def halo_copies(
    src, own, packed, halo, above, below, strip, sends, recvs, height, breadth, here, grid
):
    row, col = here
    rows, cols = grid
    up, down = lax.rem(row + rows - 1, rows), lax.rem(row + 1, rows)
    left, right = lax.rem(col + cols - 1, cols), lax.rem(col + 1, cols)
    wide = 3 * breadth
    tall = 4 * height
    corner = 8 * height

    def copy(k, source, target, device):
        return pltpu.make_async_remote_copy(
            src_ref=source,
            dst_ref=target,
            send_sem=sends.at[k],
            recv_sem=recvs.at[k],
            device_id=device,
            device_id_type=MESH,
        )

    tokens = height * breadth
    straight = [
        copy(
            0,
            src.at[pl.ds(own, wide)],
            halo.at[pl.ds(below, wide)],
            (up, col),
        ),
        copy(
            1,
            src.at[pl.ds(own + tokens - wide, wide)],
            halo.at[pl.ds(above, wide)],
            (down, col),
        ),
    ]
    around = []
    spans = [
        (0, tall, (row, left)),
        (tall, tall, (row, right)),
        (corner, 16, (up, left)),
        (corner + 16, 16, (up, right)),
        (corner + 32, 16, (down, left)),
        (corner + 48, 16, (down, right)),
    ]
    for k, (first, count, device) in enumerate(spans):
        around.append(
            copy(
                2 + k,
                packed.at[pl.ds(first, count)],
                halo.at[pl.ds(strip + first, count)],
                device,
            )
        )
    return straight, around


def transposed(values):
    return values.astype(F32).T.astype(BF16)


def soften(parts):
    top = jnp.max(parts[0], axis=0, keepdims=True)
    for part in parts[1:]:
        top = jnp.maximum(top, jnp.max(part, axis=0, keepdims=True))
    weights = [jnp.exp(part - top) for part in parts]
    total = jnp.sum(weights[0], axis=0, keepdims=True)
    for weight in weights[1:]:
        total = total + jnp.sum(weight, axis=0, keepdims=True)
    return [weight.astype(BF16) for weight in weights], 1.0 / total


def stack_heads(queries):
    lane_head = iota((1, GROUP), 1) // HEAD
    return jnp.concatenate(
        [queries * jnp.where(lane_head == h, 1.0, 0.0).astype(BF16) for h in range(GROUP // HEAD)],
        axis=0,
    )


def head_sums(terms, count):
    blocks = []
    for pair in range(GROUP // HEAD // 2):
        rows = slice(pair * 2 * HEAD, (pair + 1) * 2 * HEAD)
        lanes = slice(pair * 2 * count, (pair + 1) * 2 * count)
        both = None
        for values, weights in terms:
            term = dot(values[rows], weights[:, lanes])
            both = term if both is None else both + term
        blocks += [both[:HEAD, :count], both[HEAD:, count:]]
    return blocks


def scaled(blocks, factor, count):
    return [block * factor[:, h * count : (h + 1) * count] for h, block in enumerate(blocks)]


def inside_grid(key_row, key_col, height, breadth, here, grid):
    first_row, first_col = here[0] * height, here[1] * breadth
    return (
        (first_row + key_row >= 0)
        & (first_row + key_row < grid[0] * height)
        & (first_col + key_col >= 0)
        & (first_col + key_col < grid[1] * breadth)
    )


def fine_bias(bias_ref, height, breadth, here, grid):
    own, rows, queries = height * breadth, 4 * breadth, 2 * breadth
    k = iota((own, queries), 0)
    q = iota((own, queries), 1)
    row_gap = k // breadth - q // breadth
    near = jnp.abs(k % breadth - q % breadth) <= REACH
    index = iota((rows, 1), 0)
    query = iota((1, queries), 1)
    halo_near = jnp.abs(index % breadth - query % breadth) <= REACH
    _, _, strip_row, strip_col, valid = strip_places(iota((STRIP, 1), 0), height, breadth)
    inside = valid & inside_grid(strip_row, strip_col, height, breadth, here, grid)
    strip_near = inside & (jnp.abs(strip_col - query % breadth) <= REACH)
    for i in range(height // 2):
        first = i * (own + rows + STRIP)
        gap = row_gap - 2 * i
        seen = near & (gap >= -REACH) & (gap <= REACH)
        bias_ref[pl.ds(first, own)] = jnp.where(seen, 0.0, NEG_FILL)
        key_row = index // breadth + (-REACH if i < height // 4 else height)
        inside = (index < 3 * breadth) & inside_grid(
            key_row, index % breadth, height, breadth, here, grid
        )
        gap = key_row - query // breadth - 2 * i
        seen = halo_near & inside & (gap >= -REACH) & (gap <= REACH)
        bias_ref[pl.ds(first + own, rows)] = jnp.where(seen, 0.0, NEG_FILL)
        gap = strip_row - query // breadth - 2 * i
        seen = strip_near & (gap >= -REACH) & (gap <= REACH)
        bias_ref[pl.ds(first + own + rows, STRIP)] = jnp.where(seen, 0.0, NEG_FILL)


def fine_own(q_ref, k_ref, vt_ref, bias_ref, top_ref, total_ref, sum_ref, height, breadth):
    heads = GROUP // HEAD
    queries, own, rows = 2 * breadth, height * breadth, 4 * breadth

    def step(i, carry):
        first = pl.multiple_of(i * queries, queries)
        start = pl.multiple_of(i * (own + rows + STRIP), STRIP)
        score = dot_t(k_ref[:own, :], stack_heads(q_ref[pl.ds(first, queries), :]))
        score = score + jnp.concatenate([bias_ref[pl.ds(start, own)]] * heads, axis=1)
        top = jnp.max(score, axis=0, keepdims=True)
        weight = jnp.exp(score - top)
        top_ref[i] = top
        total_ref[i] = jnp.sum(weight, axis=0, keepdims=True)
        sums = head_sums([(vt_ref[:, :own], weight.astype(BF16))], queries)
        sum_ref[i] = jnp.concatenate(sums, axis=0)
        return carry

    lax.fori_loop(0, height // 2, step, 0)


def fine_rest(q_ref, k_ref, vt_ref, bias_ref, top_ref, total_ref, sum_ref, att_ref, height, breadth):
    heads = GROUP // HEAD
    queries, own, rows = 2 * breadth, height * breadth, 4 * breadth
    edge = own + 2 * rows

    def step(i, carry):
        first = pl.multiple_of(i * queries, queries)
        start = pl.multiple_of(i * (own + rows + STRIP), STRIP)
        side = pl.multiple_of(own + rows * (i // (height // 4)), STRIP)
        stacked = stack_heads(q_ref[pl.ds(first, queries), :])
        halo = dot_t(k_ref[pl.ds(side, rows), :], stacked)
        halo = halo + jnp.concatenate([bias_ref[pl.ds(start + own, rows)]] * heads, axis=1)
        strip = dot_t(k_ref[pl.ds(edge, STRIP), :], stacked)
        strip = strip + jnp.concatenate([bias_ref[pl.ds(start + own + rows, STRIP)]] * heads, axis=1)
        before = top_ref[i]
        top = jnp.maximum(before, jnp.max(halo, axis=0, keepdims=True))
        top = jnp.maximum(top, jnp.max(strip, axis=0, keepdims=True))
        ratio = jnp.exp(before - top)
        halo = jnp.exp(halo - top)
        strip = jnp.exp(strip - top)
        total = total_ref[i] * ratio + jnp.sum(halo, axis=0, keepdims=True)
        total = total + jnp.sum(strip, axis=0, keepdims=True)
        terms = [
            (vt_ref[:, pl.ds(side, rows)], halo.astype(BF16)),
            (vt_ref[:, edge : edge + STRIP], strip.astype(BF16)),
        ]
        known = sum_ref[i]
        known = [known[h * HEAD : (h + 1) * HEAD] for h in range(heads)]
        sums = [a + b for a, b in zip(scaled(known, ratio, queries), head_sums(terms, queries))]
        sums = jnp.concatenate(scaled(sums, 1.0 / total, queries), axis=0)
        att_ref[pl.ds(first, queries), :] = sums.T.astype(BF16)
        return carry

    lax.fori_loop(0, height // 2, step, 0)


def mid_bias(height, breadth, here, grid):
    block = height * breadth
    wide = 3 * breadth
    k = iota((4 * block, 1), 0)
    part = k // block
    index = k % block
    row, col = index // breadth, index % breadth
    _, _, strip_row, strip_col, strip_valid = strip_places(index, height, breadth)
    is_strip = part == 3
    shift = jnp.where(part == 1, -REACH, jnp.where(part == 2, height, 0))
    key_row = jnp.where(is_strip, strip_row, row + shift)
    key_col = jnp.where(is_strip, strip_col, col)
    valid = (is_strip & strip_valid) | ((part == 0) | (~is_strip & (index < wide)))
    valid = valid & inside_grid(key_row, key_col, height, breadth, here, grid)
    q = iota((1, block), 1)
    near = (jnp.abs(key_row - q // breadth) <= REACH) & (jnp.abs(key_col - q % breadth) <= REACH)
    return jnp.where(valid & near, 0.0, NEG_FILL)


def mid_attention(q_ref, k_ref, vt_ref, bias_ref, att_ref):
    count, channels = q_ref.shape
    heads = GROUP // HEAD
    for g in range(channels // GROUP):
        lanes = slice(g * GROUP, (g + 1) * GROUP)
        score = dot_t(k_ref[:, lanes], stack_heads(q_ref[:, lanes]))
        score = score + jnp.concatenate([bias_ref[...]] * heads, axis=1)
        (weight,), inverse = soften([score])
        sums = scaled(head_sums([(vt_ref[lanes, :], weight)], count), inverse, count)
        att_ref[:, lanes] = jnp.concatenate(sums, axis=0).T.astype(BF16)


def kernel(
    sizes,
    image,
    gain1,
    qkv1,
    out1,
    merge1,
    gain2,
    qkv2,
    out2,
    merge2,
    gain3,
    qkv3,
    out3,
    skip1,
    skip2,
    last,
    w_qkv1,
    w_out1,
    w_merge1,
    w_qkv2,
    w_out2,
    w_merge2,
    w_qkv3,
    w_out3,
    g1,
    g2,
    g3,
    x1,
    pack1,
    turned1,
    q1,
    k1,
    vt1,
    att1,
    bias1,
    top1,
    total1,
    sum1,
    x2,
    pack2,
    turned2,
    q2,
    k2,
    vt2,
    att2,
    bias2,
    merge_pick1,
    merge_pick2,
    strip_pick2,
    x3,
    head_out,
    head_in,
    kv_all,
    top,
    total,
    acc,
    back_out,
    back_in,
    att3,
    load_sem,
    halo1_send,
    halo1_recv,
    halo2_send,
    halo2_recv,
    head_send,
    head_recv,
    far_send,
    pair_send,
    kv_recv,
    back_send,
    back_recv,
    plane_sem,
):
    h1, c1, h2, c2, t3, rows, cols = sizes
    grid = (rows, cols)
    row, col = lax.axis_index("row"), lax.axis_index("col")
    here = (row, col)
    members, around = len(NEAR), len(FAR)
    core = lax.rem(row, CORES)
    spot = (
        lax.rem(row // CORES, SIDE),
        col // 2,
        lax.rem(col, 2) * 2 + row // (CORES * SIDE),
    )

    def chip(*shifts):
        return tuple(
            lax.rem(spot[d] + sum(shift[d] for shift in shifts) % SIDE, SIDE) for d in range(3)
        )

    def device(place):
        x, y, z = place
        return (lax.rem(z, 2) * (SIDE * CORES) + x * CORES + core, y * 2 + z // 2)

    def head_of(place):
        x, y, z = place
        high = lax.rem(x // 2 + y // 2 + z // 2, 2)
        return lax.rem(x, 2) + 2 * lax.rem(y, 2) + 4 * lax.rem(z, 2) + 8 * high

    def back_along(shift):
        return tuple(-step % SIDE for step in shift)

    mine = head_of(spot)
    other = (row - core + (CORES - 1) - core, col)

    loads = [
        pltpu.make_async_copy(src, dst, load_sem.at[k])
        for k, (src, dst) in enumerate(
            [
                (image, x1.at[pl.ds(0, h1 * c1)]),
                (qkv1, w_qkv1),
                (out1, w_out1),
                (merge1, w_merge1),
                (qkv2, w_qkv2),
                (out2, w_out2),
                (merge2, w_merge2),
                (qkv3, w_qkv3),
                (out3, w_out3),
                (gain1, g1),
                (gain2, g2),
                (gain3, g3),
            ]
        )
    ]
    early = (0, 1, 9)
    for k in early:
        loads[k].start()

    barrier = pltpu.get_barrier_semaphore()

    def greet(device):
        pl.semaphore_signal(barrier, inc=1, device_id=device, device_id_type=MESH)

    for down in (rows - 1, 0, 1):
        for right in (cols - 1, 0, 1):
            if down or right:
                greet((lax.rem(row + down, rows), lax.rem(col + right, cols)))
    around_here = sorted({shift for near in NEAR[1:] for shift in (near, back_along(near))})
    for shift in around_here + list(FAR[1:]):
        greet(device(chip(shift)))
    greet(other)

    n1, n2 = h1 * c1, h2 * c2
    w1, w2 = x1.shape[1], x2.shape[1]
    above1, below1, edge1 = n1, n1 + 4 * c1, n1 + 8 * c1
    for first in (above1 + 3 * c1, below1 + 3 * c1):
        x1[pl.ds(first, c1)] = jnp.zeros((c1, w1), BF16)
    straight, edges = halo_copies(
        image, 0, pack1, x1, above1, below1, edge1, halo1_send, halo1_recv, h1, c1, here, grid
    )
    loads[0].wait()
    block = x1[pl.ds(0, n1)]
    pack1[...] = dot(strip_pick(h1, c1), block).astype(BF16)
    pl.semaphore_wait(barrier, 8 + len(around_here) + around - 1 + 1)
    for copy in edges + straight:
        copy.start()
    for far in FAR[1:]:
        pl.semaphore_signal(plane_sem, inc=1, device_id=device(chip(far)), device_id_type=MESH)
    for k, load in enumerate(loads):
        if k not in early:
            load.start()
    loads[9].wait()
    loads[1].wait()
    turned1[...] = transposed(w_qkv1[:, 2 * w1 :])
    normed = rms_norm(block, g1[...])
    projected = dot(normed, w_qkv1[:, : 2 * w1])
    q1[...] = (projected[:, :w1] * HEAD ** (-0.5)).astype(BF16)
    k1[pl.ds(0, n1)] = projected[:, w1:].astype(BF16)
    vt1[:, :n1] = dot_t(turned1[...], normed).astype(BF16)
    fine_bias(bias1, h1, c1, here, grid)
    merge_pick1[...] = merge_pick(n1, c1)
    merge_pick2[...] = merge_pick(n2, c2)
    strip_pick2[...] = strip_pick(h2, c2)
    for first in (n2 + 3 * c2, 2 * n2 + 3 * c2):
        x2[pl.ds(first, n2 - 3 * c2)] = jnp.zeros((n2 - 3 * c2, w2), BF16)
    used = 3 * n2 + 8 * h2 + 64
    x2[pl.ds(used, 4 * n2 - used)] = jnp.zeros((4 * n2 - used, w2), BF16)
    fine_own(q1, k1, vt1, bias1, top1, total1, sum1, h1, c1)
    for copy in straight + edges:
        copy.wait_recv()
    normed = rms_norm(x1[pl.ds(n1, 8 * c1 + STRIP)], g1[...])
    k1[pl.ds(n1, 8 * c1 + STRIP)] = dot(normed, w_qkv1[:, w1 : 2 * w1]).astype(BF16)
    vt1[:, n1:] = dot_t(turned1[...], normed).astype(BF16)
    fine_rest(q1, k1, vt1, bias1, top1, total1, sum1, att1, h1, c1)
    loads[2].wait()
    skip1[...] = (x1[pl.ds(0, n1)].astype(F32) + dot(att1[...], w_out1[...])).astype(BF16)
    loads[3].wait()
    block = merge_blocks(skip1[...], merge_pick1[...], w_merge1)

    x2[pl.ds(0, n2)] = block
    straight2, edges2 = halo_copies(
        x2, 0, pack2, x2, n2, 2 * n2, 3 * n2, halo2_send, halo2_recv, h2, c2, here, grid
    )
    pack2[...] = dot(strip_pick2[...], block).astype(BF16)
    for copy in edges2 + straight2:
        copy.start()
    loads[10].wait()
    loads[4].wait()
    turned2[...] = transposed(w_qkv2[:, 2 * w2 :])
    bias2[...] = mid_bias(h2, c2, here, grid)
    normed = rms_norm(block, g2[...])
    projected = dot(normed, w_qkv2[:, : 2 * w2])
    q2[...] = (projected[:, :w2] * HEAD ** (-0.5)).astype(BF16)
    k2[pl.ds(0, n2)] = projected[:, w2:].astype(BF16)
    vt2[:, :n2] = dot_t(turned2[...], normed).astype(BF16)
    for copy in straight2 + edges2:
        copy.wait_recv()
    normed = rms_norm(x2[pl.ds(n2, 3 * n2)], g2[...])
    k2[pl.ds(n2, 3 * n2)] = dot(normed, w_qkv2[:, w2 : 2 * w2]).astype(BF16)
    vt2[:, n2:] = dot_t(turned2[...], normed).astype(BF16)
    mid_attention(q2, k2, vt2, bias2, att2)
    loads[5].wait()
    skip2[...] = (block.astype(F32) + dot(att2[...], w_out2[...])).astype(BF16)
    loads[6].wait()
    block = merge_blocks(skip2[...], merge_pick2[...], w_merge2)
    x3[...] = block

    channels = x3.shape[1]
    loads[11].wait()
    loads[7].wait()
    normed = rms_norm(block, g3[...])
    projected = dot(normed, w_qkv3[:, channels:])
    low = iota((1, 2 * HEAD), 1) < HEAD
    for pair in range(channels // (2 * HEAD)):
        keys = projected[:, pair * 128 : (pair + 1) * 128]
        values = projected[:, channels + pair * 128 : channels + (pair + 1) * 128]
        even = jnp.where(low, keys, pltpu.roll(values, HEAD, 1))
        odd = jnp.where(low, pltpu.roll(keys, HEAD, 1), values)
        head_out[2 * pair, t3:] = even.astype(BF16)
        head_out[2 * pair + 1, t3:] = odd.astype(BF16)

    def head_copy(j):
        place = chip(NEAR[j])
        return pltpu.make_async_remote_copy(
            src_ref=head_out.at[head_of(place)],
            dst_ref=head_in.at[j],
            send_sem=head_send.at[j],
            recv_sem=head_recv.at[j],
            device_id=device(place),
            device_id_type=MESH,
        )

    count = members * t3

    def far_copy(f, j):
        place = chip(NEAR[j], FAR[f])
        return pltpu.make_async_remote_copy(
            src_ref=head_out.at[head_of(place), pl.ds(t3, t3)],
            dst_ref=kv_all.at[f * CORES + core, j],
            send_sem=far_send.at[f],
            recv_sem=kv_recv.at[f * CORES + core],
            device_id=device(place),
            device_id_type=MESH,
        )

    def pair_copy(f):
        return pltpu.make_async_remote_copy(
            src_ref=kv_all.at[f * CORES + core],
            dst_ref=kv_all.at[f * CORES + core],
            send_sem=pair_send.at[f],
            recv_sem=kv_recv.at[f * CORES + core],
            device_id=other,
            device_id_type=MESH,
        )

    def arrival(place):
        return pltpu.make_async_remote_copy(
            src_ref=kv_all.at[place],
            dst_ref=kv_all.at[place],
            send_sem=pair_send.at[0],
            recv_sem=kv_recv.at[place],
            device_id=other,
            device_id_type=MESH,
        )

    def far_sent(f):
        return pltpu.make_async_remote_copy(
            src_ref=kv_all.at[core],
            dst_ref=kv_all.at[core],
            send_sem=far_send.at[f],
            recv_sem=kv_recv.at[core],
            device_id=other,
            device_id_type=MESH,
        )

    pl.semaphore_wait(plane_sem, around - 1)
    for f in range(1, around):
        for j in range(members):
            far_copy(f, j).start()
    projected = dot(normed, w_qkv3[:, :channels]) * HEAD ** (-0.5)
    for pair in range(channels // (2 * HEAD)):
        tile = projected[:, pair * 128 : (pair + 1) * 128]
        turned = pltpu.roll(tile, HEAD, 1)
        head_out[2 * pair, 0:t3] = jnp.where(low, tile, 0.0).astype(BF16)
        head_out[2 * pair + 1, 0:t3] = jnp.where(low, turned, 0.0).astype(BF16)
    for j in range(1, members):
        head_copy(j).start()
    head_in[0] = head_out[mine]
    top[...] = jnp.full(top.shape, NEG_FILL, F32)
    total[...] = jnp.zeros(total.shape, F32)
    acc[...] = jnp.zeros(acc.shape, F32)
    for j in range(1, members):
        head_copy(j).wait_recv()
    kv_all[core] = head_in[:, t3:, :]

    queries = head_in[:, 0:t3, :].reshape(count, 128)
    pick = jnp.where(iota((HEAD, 128), 0) + HEAD == iota((HEAD, 128), 1), 1.0, 0.0).astype(BF16)

    def absorb(places):
        blocks = [kv_all[place].reshape(count, 128) for place in places]
        scores = [dot_t(block, queries) for block in blocks]
        before = top[...]
        now = before
        for score in scores:
            now = jnp.maximum(now, jnp.max(score, axis=0, keepdims=True))
        ratio = jnp.exp(before - now)
        top[...] = now
        part, update = total[...] * ratio, acc[...] * ratio
        for score, block in zip(scores, blocks):
            weight = jnp.exp(score - now)
            part = part + jnp.sum(weight, axis=0, keepdims=True)
            update = update + dot(dot_t(pick, block).astype(BF16), weight.astype(BF16))
        total[...] = part
        acc[...] = update

    waiting = []
    for f in range(around):
        near, far = f * CORES + core, f * CORES + (CORES - 1) - core
        if f:
            arrival(near).wait_recv()
        pair_copy(f).start()
        if waiting:
            arrival(waiting[0]).wait_recv()
        absorb(waiting + [near])
        waiting = [far]
    arrival(waiting[0]).wait_recv()
    absorb(waiting)

    result = acc[...] * (1.0 / total[...])
    result = jnp.concatenate([result, result], axis=0).T
    back_out[...] = result.astype(BF16).reshape(members, t3, 128)

    def back_copy(j):
        place = chip(back_along(NEAR[j]))
        return pltpu.make_async_remote_copy(
            src_ref=back_out.at[j],
            dst_ref=back_in.at[mine],
            send_sem=back_send.at[j],
            recv_sem=back_recv.at[mine],
            device_id=device(place),
            device_id_type=MESH,
        )

    def back_arrival(j):
        place = chip(NEAR[j])
        head = head_of(place)
        return pltpu.make_async_remote_copy(
            src_ref=back_out.at[j],
            dst_ref=back_in.at[head],
            send_sem=back_send.at[j],
            recv_sem=back_recv.at[head],
            device_id=device(place),
            device_id_type=MESH,
        )

    for j in range(1, members):
        back_copy(j).start()
    back_in[mine] = back_out[0]
    for j in range(1, members):
        back_arrival(j).wait_recv()
    for pair in range(channels // (2 * HEAD)):
        even, odd = back_in[2 * pair].astype(F32), back_in[2 * pair + 1].astype(F32)
        att3[:, pair * 128 : (pair + 1) * 128] = jnp.where(low, even, odd).astype(BF16)
    loads[8].wait()
    last[...] = (x3[...].astype(F32) + dot(att3[...], w_out3[...])).astype(BF16)

    for copy in straight + edges + straight2 + edges2:
        copy.wait_send()
    for j in range(1, members):
        head_copy(j).wait_send()
        back_copy(j).wait_send()
    for f in range(around):
        if f:
            far_sent(f).wait_send()
        pair_copy(f).wait_send()


def shards(
    rows,
    cols,
    image,
    gain_fine,
    qkv_fine,
    out_fine,
    merge_fine,
    gain_mid,
    qkv_mid,
    out_mid,
    merge_mid,
    gain_coarse,
    qkv_coarse,
    out_coarse,
):
    h1, c1, w1 = image.shape
    w2, w3 = gain_mid.shape[0], gain_coarse.shape[0]
    h2, c2 = h1 // 2, c1 // 2
    h3, c3 = h2 // 2, c2 // 2
    t1, t2, t3 = h1 * c1, h2 * c2, h3 * c3
    members, around = len(NEAR), len(FAR)
    sizes = (h1, c1, h2, c2, t3, rows, cols)
    anywhere = pl.BlockSpec(memory_space=pl.ANY)

    def vmem(*shape):
        return pltpu.VMEM(shape, BF16)

    def level(tokens, width, keys, bias):
        return [
            vmem(keys, width),
            vmem(STRIP, width),
            vmem(width, width),
            vmem(tokens, width),
            vmem(keys, width),
            vmem(width, keys),
            vmem(tokens, width),
            pltpu.VMEM(bias, F32),
        ]

    def dma(*shape):
        return pltpu.SemaphoreType.DMA(shape)

    count = members * t3
    scratch = (
        [vmem(*w.shape) for w in (qkv_fine, out_fine, merge_fine, qkv_mid, out_mid, merge_mid)]
        + [vmem(*w.shape) for w in (qkv_coarse, out_coarse)]
        + [pltpu.VMEM((1, w), F32) for w in (w1, w2, w3)]
        + level(t1, w1, t1 + 8 * c1 + STRIP, (h1 // 2 * (t1 + 4 * c1 + STRIP), 2 * c1))
        + [
            pltpu.VMEM((h1 // 2, 1, w1 // HEAD * 2 * c1), F32),
            pltpu.VMEM((h1 // 2, 1, w1 // HEAD * 2 * c1), F32),
            pltpu.VMEM((h1 // 2, w1, 2 * c1), F32),
        ]
        + level(t2, w2, 4 * t2, (4 * t2, t2))
        + [vmem(t1, t1), vmem(t2, t2), vmem(STRIP, t2)]
        + [
            vmem(t3, w3),
            vmem(members, 2 * t3, 128),
            vmem(members, 2 * t3, 128),
            vmem(CORES * around, members, t3, 128),
            pltpu.VMEM((1, count), F32),
            pltpu.VMEM((1, count), F32),
            pltpu.VMEM((HEAD, count), F32),
            vmem(members, t3, 128),
            vmem(members, t3, 128),
            vmem(t3, w3),
        ]
        + [dma(12), dma(8), dma(8), dma(8), dma(8)]
        + [dma(members), dma(members), dma(around), dma(around), dma(CORES * around)]
        + [dma(members), dma(members), pltpu.SemaphoreType.REGULAR]
    )
    skip_fine, skip_mid, coarse_out = pl.pallas_call(
        functools.partial(kernel, sizes),
        out_shape=(vmem(t1, w1), vmem(t2, w2), vmem(t3, w3)),
        in_specs=[pl.BlockSpec(memory_space=pltpu.HBM)] * 12,
        out_specs=(pl.BlockSpec(memory_space=pltpu.VMEM),) * 3,
        scratch_shapes=scratch,
        compiler_params=pltpu.CompilerParams(
            collective_id=0, has_side_effects=True, vmem_limit_bytes=60 * 1024 * 1024
        ),
    )(
        image.reshape(t1, w1),
        gain_fine.reshape(1, w1),
        qkv_fine,
        out_fine,
        merge_fine,
        gain_mid.reshape(1, w2),
        qkv_mid,
        out_mid,
        merge_mid,
        gain_coarse.reshape(1, w3),
        qkv_coarse,
        out_coarse,
    )
    return (
        skip_fine.reshape(h1, c1, w1),
        skip_mid.reshape(h2, c2, w2),
        coarse_out.reshape(h3, c3, w3),
    )


def solution(mesh):
    placed = (P("row", "col", None),) + (P(),) * 11
    rows, cols = mesh.shape["row"], mesh.shape["col"]
    return jax.shard_map(
        functools.partial(shards, rows, cols),
        mesh=mesh,
        in_specs=placed,
        out_specs=(P("row", "col", None),) * 3,
        check_vma=False,
    )
```
